256 devices in a mesh: face: 8 (over x, core), patch: 32 (over y, z).
Axes of the slice: x: 4, y: 4, z: 8, core: 2. Of those that a mesh axis runs over, the one named last changes fastest.
Arguments:
- nodes: float32 [131072, 512], P(('face', 'patch')), may hold values from -6 to 6
- edges: bfloat16 [1048576, 512], P(('face', 'patch')), may hold values from -6 to 6
- sender: int32 [1048576], P(('face', 'patch')), may hold values from 0 to 8959, as said below
- receiver: int32 [1048576], P(('face', 'patch')), may hold values from 0 to 512, as said below
- send_rows: int32 [1024, 64], P(('face', 'patch')), may hold values from 0 to 511
- w_sender: bfloat16 [512, 512], replicated, may hold values from -0.25 to 0.25
- w_receiver: bfloat16 [512, 512], replicated, may hold values from -0.25 to 0.25
- w_edge: bfloat16 [512, 512], replicated, may hold values from -0.25 to 0.25
- bias_edge1: float32 [512], replicated, may hold values from -3 to 3
- w_edge2: bfloat16 [512, 512], replicated, may hold values from -0.25 to 0.25
- bias_edge2: float32 [512], replicated, may hold values from -3 to 3
- gain_edge: float32 [512], replicated, may hold values from 0.1 to 1.9
- shift_edge: float32 [512], replicated, may hold values from -3 to 3
- w_node_self: bfloat16 [512, 512], replicated, may hold values from -0.25 to 0.25
- w_node_aggr: bfloat16 [512, 512], replicated, may hold values from -0.25 to 0.25
- bias_node1: float32 [512], replicated, may hold values from -3 to 3
- w_node2: bfloat16 [512, 512], replicated, may hold values from -0.25 to 0.25
- bias_node2: float32 [512], replicated, may hold values from -3 to 3
- gain_node: float32 [512], replicated, may hold values from 0.1 to 1.9
- shift_node: float32 [512], replicated, may hold values from -3 to 3
Outputs:
- new_nodes: float32 [131072, 512], P(('face', 'patch'))
- new_edges: bfloat16 [1048576, 512], P(('face', 'patch'))
The draws below stay inside these ranges and needn't reach their ends.
Inputs may be any that keep to these rules, and one draw needn't show every extreme that they name: `sender`: rows below 512 are the device's own nodes, the next 256 its halo, the rest the coarse rows. `receiver`: within each device's slots the receivers never fall; empty slots come last and carry 512.
All inputs are finite; a program needn't handle non-finite values.
Results may differ from the reference program's by a relative error of at most 0.0055.
Values may be sent and summed in bfloat16 or wider, within the bound.
No kernel may reach another device: no remote copies, remote signals or barrier semaphores. Data moves between devices by JAX's collectives and lax.ppermute only.
A program may use at most 128 MiB of HBM per device.

```python
import jax
import jax.numpy as jnp
from jax import lax

D = 512
NODE_DEV = 512
COARSE_DEV = 32
EDGE_DEV = 4096
HALO = 64
NODES = 131072
EDGES = 1048576
TABLE = 8960
N_FACE = 8
N_PATCH = 32


def draw_sender(key, part):
    key = jax.random.fold_in(key, 11)
    keys = jax.random.split(key, 4)
    coarse_rows = TABLE - NODE_DEV - 4 * HALO
    kinds = jax.random.randint(keys[0], (EDGES,), 0, 20)
    local = jax.random.randint(keys[1], (EDGES,), 0, NODE_DEV)
    rim = NODE_DEV + jax.random.randint(keys[2], (EDGES,), 0, 4 * HALO)
    far = NODE_DEV + 4 * HALO + jax.random.randint(keys[3], (EDGES,), 0, coarse_rows)
    picks = jnp.where(kinds < 12, local, jnp.where(kinds < 17, rim, far))
    picks = picks.at[0].set(0)
    return picks.at[EDGES - 1].set(TABLE - 1).astype(jnp.int32)


def draw_receiver(key, part):
    key = jax.random.fold_in(key, 23)
    keys = jax.random.split(key, 2)
    count = EDGES // EDGE_DEV
    live = jax.random.randint(keys[0], (count,), EDGE_DEV // 2, EDGE_DEV + 1)
    live = live.at[0].set(EDGE_DEV)
    live = live.at[count - 1].set(EDGE_DEV // 2)
    ids = jnp.sort(jax.random.randint(keys[1], (count, EDGE_DEV), 0, NODE_DEV), axis=1)
    slots = jnp.arange(EDGE_DEV, dtype=jnp.int32)
    values = jnp.where(slots[None, :] < live[:, None], ids, NODE_DEV)
    return values.reshape(EDGES).astype(jnp.int32)


def plant(result, stream_key, least, largest):
    place = [jax.random.randint(jax.random.fold_in(stream_key, axis), (), 0, length) for axis, length in enumerate(result.shape)]
    longest = result.shape.index(max(result.shape))
    neighbour = place[:longest] + [(place[longest] + 1) % result.shape[longest]] + place[longest + 1:]
    return result.at[tuple(place)].set(least).at[tuple(neighbour)].set(largest)


def block_levels(rng, shape, pieces, low, high):
    level, own = 1.0, jax.random.fold_in(rng, 6)
    for axis_at, parts in pieces:
        steps = jnp.exp(jax.random.uniform(jax.random.fold_in(own, axis_at), (parts,), jnp.float32, low / len(pieces), high / len(pieces)))
        level = level * jnp.repeat(steps, shape[axis_at] // parts).reshape([-1 if axis == axis_at else 1 for axis in range(len(shape))])
    return level


def gaussian(rng, extent, scale, limit, cuts=(), kind=jnp.bfloat16):
    result = scale * jax.random.normal(rng, extent, jnp.float32)
    if cuts:
        result = result * block_levels(rng, extent, cuts, -0.22, 0.18)
    return jnp.clip(result, -limit, limit).astype(kind)


def setup_inputs(seed: int = 0) -> dict:
    splits = jax.random.split(jax.random.key(seed), 21)
    nodes = gaussian(splits[0], (NODES, D), 1.0, 6.0, ((0, 256),), jnp.float32)
    edges = gaussian(splits[1], (EDGES, D), 1.0, 6.0, ((0, 256),))
    sender = draw_sender(jax.random.fold_in(splits[20], 71), 0)
    receiver = draw_receiver(jax.random.fold_in(splits[20], 71), 0)
    send_rows = plant(jax.random.randint(splits[4], (4 * N_FACE * N_PATCH, HALO), 0, NODE_DEV), jax.random.fold_in(splits[4], 1), 0, NODE_DEV - 1).astype(jnp.int32)
    w_sender = gaussian(splits[5], (D, D), D ** -0.5, 0.25)
    w_receiver = gaussian(splits[6], (D, D), D ** -0.5, 0.25)
    w_edge = gaussian(splits[7], (D, D), D ** -0.5, 0.25)
    bias_edge1 = gaussian(splits[8], (D,), 0.5, 3.0, (), jnp.float32)
    w_edge2 = gaussian(splits[9], (D, D), D ** -0.5, 0.25)
    bias_edge2 = gaussian(splits[10], (D,), 0.5, 3.0, (), jnp.float32)
    gain_edge = jnp.clip(1.0 + 0.18 * jax.random.normal(splits[11], (D,), jnp.float32), 0.1, 1.9)
    shift_edge = gaussian(splits[12], (D,), 0.5, 3.0, (), jnp.float32)
    w_node_self = gaussian(splits[13], (D, D), D ** -0.5, 0.25)
    w_node_aggr = gaussian(splits[14], (D, D), D ** -0.5, 0.25)
    bias_node1 = gaussian(splits[15], (D,), 0.5, 3.0, (), jnp.float32)
    w_node2 = gaussian(splits[16], (D, D), D ** -0.5, 0.25)
    bias_node2 = gaussian(splits[17], (D,), 0.5, 3.0, (), jnp.float32)
    gain_node = jnp.clip(1.0 + 0.18 * jax.random.normal(splits[18], (D,), jnp.float32), 0.1, 1.9)
    shift_node = gaussian(splits[19], (D,), 0.5, 3.0, (), jnp.float32)
    return dict(nodes=nodes, edges=edges, sender=sender, receiver=receiver, send_rows=send_rows, w_sender=w_sender, w_receiver=w_receiver, w_edge=w_edge, bias_edge1=bias_edge1, w_edge2=w_edge2, bias_edge2=bias_edge2, gain_edge=gain_edge, shift_edge=shift_edge, w_node_self=w_node_self, w_node_aggr=w_node_aggr, bias_node1=bias_node1, w_node2=w_node2, bias_node2=bias_node2, gain_node=gain_node, shift_node=shift_node)


def dotf(left, right):
    return jnp.dot(left.astype(jnp.float32), right.astype(jnp.float32), precision=lax.Precision.HIGHEST)

def layer_norm(values, gain, shift):
    center = values - lax.optimization_barrier(jnp.mean(values, axis=-1, keepdims=True))
    spread = lax.optimization_barrier(jnp.mean(center * center, axis=-1, keepdims=True))
    return center * lax.rsqrt(spread + 1e-05) * gain + shift

def reference(nodes, edges, sender, receiver, send_rows, w_sender, w_receiver, w_edge, bias_edge1, w_edge2, bias_edge2, gain_edge, shift_edge, w_node_self, w_node_aggr, bias_node1, w_node2, bias_node2, gain_node, shift_node):
    faces = N_FACE
    patches = N_PATCH
    count = faces * patches
    node_bf = nodes.astype(jnp.bfloat16).reshape(faces, patches, NODE_DEV, D)
    rows = send_rows.reshape(faces, patches, 4, HALO)
    outgoing = jax.vmap(jax.vmap(lambda block, picks: block[picks]))(node_bf, rows)
    halo = jnp.concatenate([jnp.roll(outgoing[:, :, 0], 1, axis=1), jnp.roll(outgoing[:, :, 1], -1, axis=1), jnp.roll(outgoing[:, :, 2], 1, axis=0), jnp.roll(outgoing[:, :, 3], -1, axis=0)], axis=2).reshape(count, 4 * HALO, D)
    coarse = node_bf[:, :, :COARSE_DEV].reshape(count * COARSE_DEV, D)
    targets = jnp.arange(NODE_DEV, dtype=jnp.int32)

    def device_step(items):
        node, edge, snd, rcv, halo_rows = items
        own_bf = node.astype(jnp.bfloat16)
        table = jnp.concatenate([own_bf, halo_rows, coarse], axis=0)
        sender_term = dotf(table[snd], w_sender)
        recv_term = dotf(own_bf, w_receiver)[jnp.minimum(rcv, NODE_DEV - 1)]
        pre = sender_term + recv_term + dotf(edge, w_edge) + bias_edge1
        hidden = jax.nn.silu(pre).astype(jnp.bfloat16)
        update = layer_norm(dotf(hidden, w_edge2) + bias_edge2, gain_edge, shift_edge)
        new_edge = (edge.astype(jnp.float32) + update).astype(jnp.bfloat16)
        onehot = (rcv[None, :] == targets[:, None]).astype(jnp.float32)
        aggregate = dotf(onehot, update.astype(jnp.bfloat16)).astype(jnp.bfloat16)
        inner = jax.nn.silu(dotf(own_bf, w_node_self) + dotf(aggregate, w_node_aggr) + bias_node1).astype(jnp.bfloat16)
        new_node = node + layer_norm(dotf(inner, w_node2) + bias_node2, gain_node, shift_node)
        return (new_node, new_edge)
    new_nodes, new_edges = lax.map(device_step, (nodes.reshape(count, NODE_DEV, D), edges.reshape(count, EDGE_DEV, D), sender.reshape(count, EDGE_DEV), receiver.reshape(count, EDGE_DEV), halo))
    return (new_nodes.reshape(NODES, D), new_edges.reshape(EDGES, D))
```

```python
import numpy as np
import jax
import jax.numpy as jnp
from jax import lax
from jax.experimental import pallas as pl
from jax.experimental.pallas import tpu as pltpu
from jax.sharding import Mesh, PartitionSpec as P

AXES = ("x", "core", "y", "z")
SIZES = (4, 2, 4, 8)
NODE = 512
HALO = 64
NEAR = NODE + 4 * HALO
COARSE_DEV = 32
D = 512
EDGE = 4096
TILE = 512
TILES = EDGE // TILE
BLOCK = 256
BLOCKS = EDGE // BLOCK
F32 = jnp.float32
BF16 = jnp.bfloat16

STAGES = (
    (((0, 0, 4),) * 2, ((2, 2, 0),) * 2, ((2, 2, 4),) * 2),
    (((1, 1, 1),) * 2, ((-1, -1, -1),) * 2, ((0, 0, 2), (0, 0, -2))),
    (((-1, 1, 1), (1, -1, -1)),),
)
LAST = (((1, 0, 0), (-1, 0, 0)), ((0, 1, 0), (0, -1, 0)), ((0, 0, 1), (0, 0, -1)))


def places():
    own = np.zeros((2, 128), np.int32)
    for core in range(2):
        held = [(0, 0, 0)]
        for stage in STAGES + (LAST,):
            held = [
                ((a[0] + o[0]) % 4, (a[1] + o[1]) % 4, (a[2] + o[2]) % 8)
                for o in [(0, 0, 0)] + [pair[core] for pair in stage]
                for a in held
            ]
        assert len(set(held)) == 128
        for block, (x, y, z) in enumerate(held):
            own[core, x * 32 + y * 8 + z] = block
    return np.stack([np.stack([own[c] if c == k else 128 + own[k] for k in range(2)]) for c in range(2)])


PLACES = places()


def device(x, c, y, z):
    return ((x % 4) * 2 + c % 2) * 32 + (y % 4) * 8 + z % 8


def receive(block, source):
    spots = [(x, c, y, z) for x in range(4) for c in range(2) for y in range(4) for z in range(8)]
    return lax.ppermute(block, AXES, [(device(*source(*spot)), device(*spot)) for spot in spots])


def from_chip(block, pair):
    return receive(block, lambda x, c, y, z: (x + pair[c][0], c, y + pair[c][1], z + pair[c][2]))


def other_core(block):
    return receive(block, lambda x, c, y, z: (x, 1 - c, y, z))


def shift_patch(block, step):
    def source(x, c, y, z):
        j = (y * 8 + z - step) % 32
        return x, c, j // 8, j % 8

    return receive(block, source)


def shift_face(block, step):
    def source(x, c, y, z):
        f = (x * 2 + c - step) % 8
        return f // 2, f % 2, y, z

    return receive(block, source)


def dot(a, b):
    return jnp.dot(a, b, preferred_element_type=F32)


def dot_first(a, b):
    return lax.dot_general(a, b, (((0,), (0,)), ((), ())), preferred_element_type=F32)


def dot_last(a, b):
    return lax.dot_general(a, b, (((1,), (1,)), ((), ())), preferred_element_type=F32)


def silu(v):
    return v / (1.0 + jnp.exp(-v))


def layer_norm(v, gain, shift):
    center = v - jnp.mean(v, axis=-1, keepdims=True)
    spread = jnp.mean(center * center, axis=-1, keepdims=True)
    return center * lax.rsqrt(spread + 1e-05) * gain + shift


def iota(shape, dim):
    return lax.broadcasted_iota(jnp.int32, shape, dim)


def pick_kernel(nodes_ref, rows_ref, own_ref, out_ref):
    own = nodes_ref[...].astype(BF16)
    own_ref[...] = own
    hot = (iota((NODE, 4 * HALO), 0) == rows_ref[...]).astype(BF16)
    out_ref[...] = dot_first(hot, own).astype(BF16)


def near_kernel(
    snd_ref, rcv_ref, code_ref, edges_ref, own_ref, h0_ref, h1_ref, h2_ref, h3_ref,
    w_sender_ref, w_receiver_ref, w_edge_ref, b1_ref, w2_ref, b2_ref, gain_ref, shift_ref,
    new_edges_ref, agg_ref, slot_ref, info_ref, code_out_ref, rcv_out_ref, far_edges_ref, far_pre_ref,
    ts, tr, upper, far_edges, far_meta, pre_buf, count, sems,
):
    t = pl.program_id(0)

    @pl.when(t == 0)
    def _():
        w_sender = w_sender_ref[...]
        ts[:NODE] = dot(own_ref[...], w_sender).astype(BF16)
        for k, h_ref in enumerate((h0_ref, h1_ref, h2_ref, h3_ref)):
            ts[NODE + k * HALO:NODE + (k + 1) * HALO] = dot(h_ref[...], w_sender).astype(BF16)
        tr[...] = dot(own_ref[...], w_receiver_ref[...]).astype(BF16)
        upper[...] = (iota((TILE, TILE), 0) < iota((TILE, TILE), 1)).astype(BF16)
        far_edges[...] = jnp.zeros_like(far_edges)
        far_meta[...] = jnp.zeros_like(far_meta)
        agg_ref[...] = jnp.zeros_like(agg_ref)
        count[0] = 0

    snd = snd_ref[0]
    rcv = rcv_ref[0]
    code = code_ref[0]
    far = snd >= NEAR
    far_f = far.astype(F32)
    both = jnp.concatenate([snd, rcv, snd, rcv, snd, rcv, snd, rcv], axis=0)
    cols = jnp.transpose(both.astype(F32), (1, 0)).astype(jnp.int32)
    snd_c = cols[:, 0:1]
    rcv_c = jnp.minimum(cols[:, 1:2], NODE - 1)

    edges = edges_ref[...]
    hot_s = (iota((TILE, NEAR), 1) == snd_c).astype(BF16)
    hot_r = (iota((TILE, NODE), 1) == rcv_c).astype(BF16)
    pre = dot(edges, w_edge_ref[...]) + dot(hot_s, ts[...]) + dot(hot_r, tr[...]) + b1_ref[...]
    hidden = silu(pre).astype(BF16)
    update = layer_norm(dot(hidden, w2_ref[...]) + b2_ref[...], gain_ref[...], shift_ref[...])
    new = edges.astype(F32) + update
    new_edges_ref[...] = jnp.where(snd_c < NEAR, new, 0.0).astype(BF16)
    hot_n = (iota((NODE, TILE), 0) == jnp.where(far, -1, rcv)).astype(BF16)
    agg_ref[...] += dot(hot_n, update.astype(BF16))

    base = count[0]
    before = dot(jnp.broadcast_to(far_f, (8, TILE)).astype(BF16), upper[...])[0:1].astype(jnp.int32)
    number = jnp.sum(far_f).astype(jnp.int32)
    slot = jnp.where(far, base + before, -1)
    slot_ref[0] = slot
    info_ref[t] = base
    count[0] = base + number
    first = base // BLOCK
    last = jnp.where(number > 0, (base + number - 1) // BLOCK + 1, first)
    zero = jnp.zeros_like(code)
    meta = jnp.concatenate([code // 128, code % 128, rcv // 128, rcv % 128, zero, zero, zero, zero], axis=0)
    meta = meta.astype(F32).astype(BF16)

    def gather(b, carry):
        hot = (iota((BLOCK, TILE), 0) + b * BLOCK == slot).astype(BF16)
        rows = pl.ds(pl.multiple_of(b * BLOCK, BLOCK), BLOCK)
        far_edges[rows] = far_edges[rows] + dot(hot, edges).astype(BF16)
        far_meta[b] = far_meta[b] + dot_last(meta, hot)
        return carry

    lax.fori_loop(first, last, gather, 0)

    @pl.when(t == TILES - 1)
    def _():
        total = count[0]
        info_ref[TILES] = total

        def finish(b, carry):
            info = far_meta[b].astype(jnp.int32)
            code_b = info[0:1] * 128 + info[1:2]
            live = iota((1, BLOCK), 1) + b * BLOCK < total
            rcv_b = jnp.where(live, info[2:3] * 128 + info[3:4], NODE)
            code_out_ref[b] = code_b
            rcv_out_ref[b] = rcv_b
            return carry

        lax.fori_loop(0, BLOCKS, finish, 0)

        def push(b, carry):
            rows = pl.ds(pl.multiple_of(b * BLOCK, BLOCK), BLOCK)
            hot = (iota((NODE, BLOCK), 0) == jnp.minimum(rcv_out_ref[b], NODE - 1)).astype(BF16)
            pre_buf[...] = dot(far_edges[rows], w_edge_ref[...]) + dot_first(hot, tr[...]) + b1_ref[...]
            one = pltpu.make_async_copy(far_edges.at[rows], far_edges_ref.at[rows], sems.at[0])
            two = pltpu.make_async_copy(pre_buf, far_pre_ref.at[rows], sems.at[1])
            one.start()
            two.start()
            one.wait()
            two.wait()
            return carry

        lax.fori_loop(0, (total + BLOCK - 1) // BLOCK, push, 0)


def far_kernel(
    info_ref, code_ref, place_ref,
    *refs,
):
    pieces = refs[:8]
    (
        near_ref, slot_ref, rcv_ref, far_edges_ref, far_pre_ref, agg_ref, nodes_ref,
        w_sender_ref, w2_ref, b2_ref, gain_ref, shift_ref,
        w_self_ref, w_aggr_ref, bn1_ref, wn2_ref, bn2_ref, gain_n_ref, shift_n_ref,
        new_nodes_ref, new_edges_ref,
        table, rows_buf, edges_buf, pre_buf, new_far, agg, sems, row_sems,
    ) = refs[8:]
    t = pl.program_id(0)

    @pl.when(t == 0)
    def _():
        copies = [
            pltpu.make_async_copy(piece, table.at[k * 1024:(k + 1) * 1024], sems.at[k])
            for k, piece in enumerate(pieces)
        ]
        for copy in copies:
            copy.start()
        agg[...] = agg_ref[...]
        inner_self = dot(nodes_ref[...].astype(BF16), w_self_ref[...]) + bn1_ref[...]
        total = info_ref[TILES]
        for copy in copies:
            copy.wait()

        def block(b, carry):
            rows = pl.ds(pl.multiple_of(b * BLOCK, BLOCK), BLOCK)
            one = pltpu.make_async_copy(far_edges_ref.at[rows], edges_buf, row_sems.at[0])
            two = pltpu.make_async_copy(far_pre_ref.at[rows], pre_buf, row_sems.at[1])
            one.start()
            two.start()

            def gather(i, c):
                for k in range(8):
                    slot = i * 8 + k
                    code = code_ref[b * BLOCK + slot]
                    place = place_ref[code // 32] * 32 + code % 32
                    rows_buf[pl.ds(pl.multiple_of(slot * 4, 4), 4)] = table[place].astype(F32)
                return c

            lax.fori_loop(0, BLOCK // 8, gather, 0)
            sent = jnp.concatenate(
                [rows_buf[pl.ds(k, BLOCK, stride=4)] for k in range(4)], axis=1
            ).astype(BF16)
            one.wait()
            two.wait()
            pre = pre_buf[...] + dot(sent, w_sender_ref[...])
            hidden = silu(pre).astype(BF16)
            update = layer_norm(dot(hidden, w2_ref[...]) + b2_ref[...], gain_ref[...], shift_ref[...])
            new_far[rows] = (edges_buf[...].astype(F32) + update).astype(BF16)
            hot = (iota((NODE, BLOCK), 0) == rcv_ref[b]).astype(BF16)
            agg[...] += dot(hot, update.astype(BF16))
            return carry

        lax.fori_loop(0, (total + BLOCK - 1) // BLOCK, block, 0)
        aggregate = agg[...].astype(BF16)
        inner = silu(inner_self + dot(aggregate, w_aggr_ref[...])).astype(BF16)
        out = layer_norm(dot(inner, wn2_ref[...]) + bn2_ref[...], gain_n_ref[...], shift_n_ref[...])
        new_nodes_ref[...] = nodes_ref[...] + out

    base = info_ref[t]
    end = info_ref[t + 1]
    first = base // BLOCK
    last = jnp.where(end > base, (end - 1) // BLOCK + 1, first)
    new_edges_ref[...] = near_ref[...]

    def scatter(b, carry):
        hot = (iota((BLOCK, TILE), 0) + b * BLOCK == slot_ref[0]).astype(BF16)
        rows = pl.ds(pl.multiple_of(b * BLOCK, BLOCK), BLOCK)
        new_edges_ref[...] = new_edges_ref[...] + dot_first(hot, new_far[rows]).astype(BF16)
        return carry

    lax.fori_loop(first, last, scatter, 0)


def full(shape):
    return pl.BlockSpec(shape, lambda *_: (0,) * len(shape))


ANY = pl.BlockSpec(memory_space=pl.ANY)
SMEM = pl.BlockSpec(memory_space=pltpu.SMEM)
ROW = pl.BlockSpec((1, 1, TILE), lambda t: (t, 0, 0))
EDGES = pl.BlockSpec((TILE, D), lambda t: (t, 0))
SQUARE = full((D, D))
VECTOR = full((1, D))


def shape(dims, kind):
    return jax.ShapeDtypeStruct(dims, kind)


def pick(nodes, send_rows):
    return pl.pallas_call(
        pick_kernel,
        out_shape=(shape((NODE, D), BF16), shape((4 * HALO, D), BF16)),
        compiler_params=pltpu.CompilerParams(vmem_limit_bytes=16 << 20),
        cost_estimate=pl.CostEstimate(flops=2 * NODE * D * 256, bytes_accessed=2 << 20, transcendentals=0),
    )(nodes, send_rows.reshape(1, 4 * HALO))


def near(snd, rcv, code, edges, own, halo, w_sender, w_receiver, w_edge, b1, w2, b2, gain, shift):
    return pl.pallas_call(
        near_kernel,
        grid=(TILES,),
        in_specs=[ROW, ROW, ROW, EDGES, SQUARE] + [full((HALO, D))] * 4
        + [SQUARE, SQUARE, SQUARE, VECTOR, SQUARE, VECTOR, VECTOR, VECTOR],
        out_specs=[
            EDGES, SQUARE, ROW, SMEM, full((BLOCKS, 1, BLOCK)), full((BLOCKS, 1, BLOCK)), ANY, ANY,
        ],
        out_shape=(
            shape((EDGE, D), BF16), shape((NODE, D), F32), shape((TILES, 1, TILE), jnp.int32),
            shape((16,), jnp.int32),
            shape((BLOCKS, 1, BLOCK), jnp.int32), shape((BLOCKS, 1, BLOCK), jnp.int32),
            shape((EDGE, D), BF16), shape((EDGE, D), F32),
        ),
        scratch_shapes=[
            pltpu.VMEM((NEAR, D), BF16), pltpu.VMEM((NODE, D), BF16), pltpu.VMEM((TILE, TILE), BF16),
            pltpu.VMEM((EDGE, D), BF16), pltpu.VMEM((BLOCKS, 8, BLOCK), F32), pltpu.VMEM((BLOCK, D), F32),
            pltpu.SMEM((1,), jnp.int32), pltpu.SemaphoreType.DMA((2,)),
        ],
        compiler_params=pltpu.CompilerParams(vmem_limit_bytes=40 << 20),
        cost_estimate=pl.CostEstimate(flops=14 << 30, bytes_accessed=20 << 20, transcendentals=4 << 20),
    )(snd, rcv, code, edges, own, *halo, w_sender, w_receiver, w_edge, b1, w2, b2, gain, shift)


def far(info, code, place, pieces, near_edges, slot, rcv, far_edges, far_pre, agg, nodes, *weights):
    return pl.pallas_call(
        far_kernel,
        grid_spec=pltpu.PrefetchScalarGridSpec(
            num_scalar_prefetch=3,
            grid=(TILES,),
            in_specs=[ANY] * 8
            + [pl.BlockSpec((TILE, D), lambda t, *_: (t, 0)), pl.BlockSpec((1, 1, TILE), lambda t, *_: (t, 0, 0)),
               full((BLOCKS, 1, BLOCK)), ANY, ANY, SQUARE, SQUARE]
            + [SQUARE, SQUARE, VECTOR, VECTOR, VECTOR]
            + [SQUARE, SQUARE, VECTOR, SQUARE, VECTOR, VECTOR, VECTOR],
            out_specs=[SQUARE, pl.BlockSpec((TILE, D), lambda t, *_: (t, 0))],
            scratch_shapes=[
                pltpu.VMEM((8192, 4, 128), BF16), pltpu.VMEM((4 * BLOCK, 128), F32),
                pltpu.VMEM((BLOCK, D), BF16), pltpu.VMEM((BLOCK, D), F32), pltpu.VMEM((EDGE, D), BF16),
                pltpu.VMEM((NODE, D), F32), pltpu.SemaphoreType.DMA((8,)), pltpu.SemaphoreType.DMA((2,)),
            ],
        ),
        out_shape=(shape((NODE, D), F32), shape((EDGE, D), BF16)),
        input_output_aliases={11: 1},
        compiler_params=pltpu.CompilerParams(vmem_limit_bytes=48 << 20),
        cost_estimate=pl.CostEstimate(flops=4 << 30, bytes_accessed=24 << 20, transcendentals=1 << 20),
    )(info, code, place, *pieces, near_edges, slot, rcv, far_edges, far_pre, agg, nodes, *weights)


def body(
    nodes, edges, sender, receiver, send_rows,
    w_sender, w_receiver, w_edge, bias_edge1, w_edge2, bias_edge2, gain_edge, shift_edge,
    w_node_self, w_node_aggr, bias_node1, w_node2, bias_node2, gain_node, shift_node,
):
    row = lambda v: v.reshape(1, D)
    x, c, y, z = (lax.axis_index(a) for a in AXES)
    held = nodes[:COARSE_DEV].astype(BF16).reshape(COARSE_DEV, 4, 128)
    own, out = pick(nodes, send_rows)
    for stage in STAGES:
        held = jnp.concatenate([held] + [from_chip(held, pair) for pair in stage], axis=0)
    halo = [
        shift_patch(out[:HALO], 1), shift_patch(out[HALO:2 * HALO], -1),
        shift_face(out[2 * HALO:3 * HALO], 1), shift_face(out[3 * HALO:], -1),
    ]
    pieces = [held] + [from_chip(held, pair) for pair in LAST]
    pieces = pieces + [other_core(piece) for piece in pieces]

    q = jnp.maximum(sender - NEAR, 0)
    p, r = q // 32, q % 32
    d = ((p // 64 - x) % 4) * 32 + ((p // 8 - y) % 4) * 8 + (p - z) % 8
    code = (((p // 32) % 2) * 128 + d) * 32 + r
    place = lax.dynamic_index_in_dim(jnp.asarray(PLACES.reshape(2, 256)), c, keepdims=False)

    tiles = lambda v: v.reshape(TILES, 1, TILE)
    near_edges, agg, slot, info, far_code, far_rcv, far_edges, far_pre = near(
        tiles(sender), tiles(receiver), tiles(code), edges, own, halo,
        w_sender, w_receiver, w_edge, row(bias_edge1), w_edge2, row(bias_edge2), row(gain_edge), row(shift_edge),
    )
    return far(
        info, far_code.reshape(EDGE), place, pieces, near_edges, slot, far_rcv, far_edges, far_pre, agg, nodes,
        w_sender, w_edge2, row(bias_edge2), row(gain_edge), row(shift_edge),
        w_node_self, w_node_aggr, row(bias_node1), w_node2, row(bias_node2), row(gain_node), row(shift_node),
    )


def solution(mesh):
    grid = Mesh(mesh.devices.reshape(SIZES), AXES)
    split = P(AXES, None)
    return jax.shard_map(
        body,
        mesh=grid,
        in_specs=(split, split, P(AXES), P(AXES), split) + (P(),) * 15,
        out_specs=(split, split),
        check_vma=False,
    )
```

```python
import functools

import numpy as np
import jax
import jax.numpy as jnp
from jax import lax
from jax.experimental import pallas as pl
from jax.experimental.pallas import tpu as pltpu
from jax.sharding import Mesh, PartitionSpec as P

AXES = ("x", "core", "y", "z")
SIZES = (4, 2, 4, 8)
NODE = 512
HALO = 64
NEAR = NODE + 4 * HALO
COARSE_DEV = 32
D = 512
EDGE = 4096
TILE = 1024
TILES = EDGE // TILE
BLOCK = 256
SLOTS = 768
BLOCKS = 18
PARTS = 4
LATE = 2
WINDOW = 240
SUB = 512
ROWS = [slice(k, k + SUB) for k in range(0, TILE, SUB)]
F32 = jnp.float32
BF16 = jnp.bfloat16

STAGES = (
    (((0, 0, 4),) * 2,),
    (((2, 0, 0), (0, 2, 0)), ((0, 2, 0), (2, 0, 0)), ((2, 2, 0),) * 2),
    (((1, 1, 1), (-1, -1, -1)), ((-1, -1, -1), (1, 1, 1)), ((0, 0, 2), (0, 0, -2))),
)
LAST = (((1, 0, 0), (-1, 0, 0)), ((0, 1, 0), (0, -1, 0)), ((0, 0, 1), (0, 0, -1)))


def places():
    own = np.zeros((2, 128), np.int32)
    for core in range(2):
        held = [(0, 0, 0)]
        for stage in STAGES + (LAST,):
            held = [
                ((a[0] + o[0]) % 4, (a[1] + o[1]) % 4, (a[2] + o[2]) % 8)
                for o in [(0, 0, 0)] + [pair[core] for pair in stage]
                for a in held
            ]
        assert len(set(held)) == 128
        for block, (x, y, z) in enumerate(held):
            own[core, x * 32 + y * 8 + z] = block
    return np.stack([np.stack([own[c] if c == k else 128 + own[k] for k in range(2)]) for c in range(2)])


PLACES = places()


def device(x, c, y, z):
    return ((x % 4) * 2 + c % 2) * 32 + (y % 4) * 8 + z % 8


def receive(block, source):
    spots = [(x, c, y, z) for x in range(4) for c in range(2) for y in range(4) for z in range(8)]
    return lax.ppermute(block, AXES, [(device(*source(*spot)), device(*spot)) for spot in spots])


def from_chip(block, pair):
    return receive(block, lambda x, c, y, z: (x + pair[c][0], c, y + pair[c][1], z + pair[c][2]))


def other_core(block):
    return receive(block, lambda x, c, y, z: (x, 1 - c, y, z))


def shift_patch(block, step):
    def source(x, c, y, z):
        j = (y * 8 + z - step) % 32
        return x, c, j // 8, j % 8

    return receive(block, source)


def next_chip(block):
    return receive(block, lambda x, c, y, z: (x - 1 + 2 * c, 1 - c, y, z))


def dot(a, b):
    return jnp.dot(a, b, preferred_element_type=F32)


def dot_first(a, b):
    return lax.dot_general(a, b, (((0,), (0,)), ((), ())), preferred_element_type=F32)


def dot_last(a, b):
    return lax.dot_general(a, b, (((1,), (1,)), ((), ())), preferred_element_type=F32)


def silu(v):
    half = 0.5 * v
    return half + half * jnp.tanh(half)


def layer_norm(v, gain, shift):
    center = v - jnp.mean(v, axis=-1, keepdims=True)
    spread = jnp.mean(center * center, axis=-1, keepdims=True)
    return center * lax.rsqrt(spread + 1e-05) * gain + shift


def iota(shape, dim):
    return lax.broadcasted_iota(jnp.int32, shape, dim)


def pick_kernel(spot_ref, nodes_ref, rows_ref, own_ref, *out_refs):
    own = nodes_ref[...].astype(BF16)
    own_ref[...] = own
    core = spot_ref[3]
    for row, out_ref in zip((0, 1, 3 - core, 2 + core), out_refs):
        hot = (iota((NODE, HALO), 0) == rows_ref[pl.ds(row, 1), :]).astype(BF16)
        out_ref[...] = dot_first(hot, own).astype(BF16)


def compact_kernel(
    spot_ref, snd_ref, rcv_ref, edges_ref, own_ref, w_sender_ref, w_receiver_ref, w_edge_ref, b1_ref, place_ref,
    slot_ref, info_ref, code_out_ref, rcv_out_ref, ts_ref, tr_ref, far_edges_ref, far_pre_ref,
    upper, far_edges, far_meta, far_pre, count, sems,
):
    ts_ref[...] = dot(own_ref[...], w_sender_ref[...]).astype(BF16)
    tr_ref[...] = dot(own_ref[...], w_receiver_ref[...]).astype(BF16)
    upper[...] = (iota((TILE, TILE), 0) < iota((TILE, TILE), 1)).astype(BF16)
    rcv_out_ref[...] = jnp.full_like(rcv_out_ref, NODE)
    count[0] = 0
    for t in range(TILES):
        compact_tile(
            t, spot_ref, snd_ref, rcv_ref, edges_ref, slot_ref, info_ref, upper, far_edges, far_meta, count,
        )
    total = count[0]
    info_ref[TILES] = total
    blocks = (total + BLOCK - 1) // BLOCK

    def copies(b):
        rows = pl.ds(pl.multiple_of(b * BLOCK, BLOCK), BLOCK)
        return (
            pltpu.make_async_copy(far_edges.at[rows], far_edges_ref.at[rows], sems.at[b, 0]),
            pltpu.make_async_copy(far_pre.at[rows], far_pre_ref.at[rows], sems.at[b, 1]),
        )

    def push(b, carry):
        info = far_meta[b].astype(jnp.int32)
        spots = (iota((256, BLOCK), 0) == info[0:1]).astype(BF16)
        block = dot(place_ref[...], spots)[0:1].astype(jnp.int32)
        code_out_ref[b] = block * 32 + info[1:2]
        live = iota((1, BLOCK), 1) + b * BLOCK < total
        rcv_b = jnp.where(live, info[2:3] * 128 + info[3:4], NODE)
        rcv_out_ref[b] = rcv_b
        rows = pl.ds(pl.multiple_of(b * BLOCK, BLOCK), BLOCK)
        hot = (iota((NODE, BLOCK), 0) == jnp.minimum(rcv_b, NODE - 1)).astype(BF16)
        far_pre[rows] = dot(far_edges[rows], w_edge_ref[...]) + dot_first(hot, tr_ref[...]) + b1_ref[...]
        for copy in copies(b):
            copy.start()
        return carry

    lax.fori_loop(0, blocks, push, 0)

    def settle(b, carry):
        for copy in copies(b):
            copy.wait()
        return carry

    lax.fori_loop(0, blocks, settle, 0)


def compact_tile(t, spot_ref, snd_ref, rcv_ref, edges_ref, slot_ref, info_ref, upper, far_edges, far_meta, count):
    rcv = rcv_ref[t]
    snd = snd_ref[t]
    far = snd >= NEAR
    q = jnp.maximum(snd - NEAR, 0)
    p = q >> 5
    dx = ((p >> 6) - spot_ref[0]) & 3
    dy = ((p >> 3) - spot_ref[1]) & 3
    dz = (p - spot_ref[2]) & 7
    place = (((p >> 5) & 1) << 7) | (dx << 5) | (dy << 3) | dz
    far_f = far.astype(F32)
    base = count[0]
    before = dot(jnp.broadcast_to(far_f, (8, TILE)).astype(BF16), upper[...])[0:1].astype(jnp.int32)
    number = jnp.sum(far_f).astype(jnp.int32)
    slot = jnp.where(far, base + before, -1)
    slot_ref[t] = slot
    info_ref[t] = base
    count[0] = base + number
    first = base // BLOCK
    last = jnp.where(number > 0, (base + number - 1) // BLOCK + 1, first)
    zero = jnp.zeros_like(rcv)
    meta = jnp.concatenate([place, q & 31, rcv >> 7, rcv & 127, zero, zero, zero, zero], axis=0)
    meta = meta.astype(F32).astype(BF16)

    def gather(b, carry):
        hot = (iota((BLOCK, TILE), 0) + b * BLOCK == slot).astype(BF16)
        rows = pl.ds(pl.multiple_of(b * BLOCK, BLOCK), BLOCK)
        fresh = b * BLOCK >= base
        far_edges[rows] = jnp.where(fresh, 0.0, far_edges[rows]) + dot(hot, edges_ref[t * TILE:(t + 1) * TILE]).astype(BF16)
        far_meta[b] = jnp.where(fresh, 0.0, far_meta[b]) + dot_last(meta, hot)
        return carry

    lax.fori_loop(first, last, gather, 0)


def near_kernel(part, pieces, *refs):
    (
        snd_ref, rcv_ref, edges_ref, tr_ref,
        w_edge_ref, b1_ref, w2_ref, b2_ref, gain_ref, shift_ref,
    ) = refs[:10]
    if part == 0:
        spot_ref, own_ts_ref, h0_ref, h1_ref, h2_ref, h3_ref, w_sender_ref = refs[10:17]
        ts_ref, new_edges_ref, agg_ref, window = refs[17:]
        w_sender = w_sender_ref[...]
        ts_ref[:NODE] = own_ts_ref[...]
        core = spot_ref[3]
        for k, h_ref in zip((0, 1, 2 + core, 3 - core), (h0_ref, h1_ref, h2_ref, h3_ref)):
            there = pl.ds(pl.multiple_of(NODE + k * HALO, HALO), HALO)
            ts_ref[there] = dot(h_ref[...], w_sender).astype(BF16)
        agg_ref[...] = jnp.zeros_like(agg_ref)
    else:
        ts_ref, sum_ref = refs[10:12]
        ready = refs[12:12 + pieces]
        new_edges_ref, agg_ref = refs[12 + pieces:14 + pieces]
        window = refs[-1 - (pieces > 0)]
        agg_ref[...] = sum_ref[...]
        copies = [
            pltpu.make_async_copy(piece, refs[14 + pieces].at[k * 1024:(k + 1) * 1024], refs[-1].at[k])
            for k, piece in enumerate(ready)
        ]
        for copy in copies:
            copy.start()
    window[WINDOW:] = tr_ref[NODE - 16:]
    offset = part * TILE

    snd = snd_ref[part]
    rcv = rcv_ref[part]
    far = snd >= NEAR
    live = rcv < NODE
    low = jnp.min(rcv)
    high = jnp.max(jnp.where(live, rcv, -1))
    start = pl.multiple_of(jnp.minimum(low // 16 * 16, NODE - WINDOW), 16)
    narrow = high - start < WINDOW

    def edge_rows(hot_of, agg_rows, agg_hot):
        updates = []
        for rows in ROWS:
            edges = edges_ref[offset + rows.start:offset + rows.stop]
            hot, table, keep = hot_of(rows)
            pre = dot(edges, w_edge_ref[...]) + b1_ref[...]
            for h, part in zip(hot, table):
                pre = pre + dot(h, part)
            hidden = silu(pre).astype(BF16)
            update = layer_norm(dot(hidden, w2_ref[...]) + b2_ref[...], gain_ref[...], shift_ref[...])
            new_edges_ref[rows] = jnp.where(keep, edges.astype(F32) + update, 0.0).astype(BF16)
            updates.append(update.astype(BF16))
        agg_ref[agg_rows] += dot(agg_hot, jnp.concatenate(updates, axis=0))

    def columns(second):
        first = jnp.where(far, -1, snd)
        both = jnp.concatenate([first, second] * 4, axis=0)
        cols = jnp.transpose(both.astype(F32), (1, 0)).astype(jnp.int32)
        return cols[:, 0:1], cols[:, 1:2]

    @pl.when(narrow)
    def _():
        window[:WINDOW] = tr_ref[pl.ds(start, WINDOW)]
        snd_c, rcv_c = columns(jnp.where(live, rcv - start, WINDOW + 15))

        def hot_of(rows):
            a = (iota((SUB, NEAR), 1) == snd_c[rows]).astype(BF16)
            b = (iota((SUB, 256), 1) == rcv_c[rows]).astype(BF16)
            return [a, b], [ts_ref[...], window[...]], snd_c[rows] >= 0

        hot_n = (iota((WINDOW, TILE), 0) == jnp.where(far, -1, rcv - start)).astype(BF16)
        edge_rows(hot_of, pl.ds(start, WINDOW), hot_n)

    @pl.when(jnp.logical_not(narrow))
    def _():
        snd_c, rcv_c = columns(jnp.minimum(rcv, NODE - 1))

        def hot_of(rows):
            a = (iota((SUB, NEAR), 1) == snd_c[rows]).astype(BF16)
            b = (iota((SUB, NODE), 1) == rcv_c[rows]).astype(BF16)
            return [a, b], [ts_ref[...], tr_ref[...]], snd_c[rows] >= 0

        hot_n = (iota((NODE, TILE), 0) == jnp.where(far, -1, rcv)).astype(BF16)
        edge_rows(hot_of, slice(None), hot_n)

    if pieces:
        for copy in copies:
            copy.wait()


def far_kernel(info_ref, code_ref, *refs):
    late = refs[1:1 + LATE]
    near_refs = refs[1 + LATE:1 + LATE + TILES]
    (
        far_edges_ref, far_pre_ref, agg_ref, slot_ref, rcv_ref, nodes_ref,
        w_sender, w2, w_self, w_aggr, wn2,
        b2_ref, gain_ref, shift_ref, bn1_ref, bn2_ref, gain_n_ref, shift_n_ref,
        new_nodes_ref, new_edges_ref, table,
        rows_buf, edges_buf, pre_buf, new_far, agg, near, sems, near_sems, row_sems,
    ) = refs[1 + LATE + TILES:]
    copies = [
        pltpu.make_async_copy(piece, table.at[(8 - LATE + k) * 1024:(9 - LATE + k) * 1024], sems.at[k])
        for k, piece in enumerate(late)
    ]

    def block_copies(b):
        rows = pl.ds(pl.multiple_of(b * SLOTS, SLOTS), SLOTS)
        return (
            pltpu.make_async_copy(far_edges_ref.at[rows], edges_buf, row_sems.at[0]),
            pltpu.make_async_copy(far_pre_ref.at[rows], pre_buf, row_sems.at[1]),
        )

    total = info_ref[TILES]
    for copy in copies:
        copy.start()

    @pl.when(total > 0)
    def _():
        for copy in block_copies(0):
            copy.start()

    agg[...] = agg_ref[...]
    inner_self = dot(nodes_ref[...].astype(BF16), w_self[...]) + bn1_ref[...]
    for copy in copies:
        copy.wait()

    def block(b, carry):
        @pl.when(b > 0)
        def _():
            for copy in block_copies(b):
                copy.start()

        count = jnp.minimum(SLOTS, (total - b * SLOTS + 15) // 16 * 16)

        row = b * (SLOTS // BLOCK)

        def gather(i, c):
            for k in range(16):
                slot = i * 16 + k
                code = code_ref[row + (slot >> 8), 0, slot & 255]
                rows_buf[pl.ds(pl.multiple_of(slot * 4, 4), 4)] = table[code].astype(F32)
            return c

        lax.fori_loop(0, count // 16, gather, 0)
        for copy in block_copies(b):
            copy.wait()
        for k in range(SLOTS // BLOCK):
            here = slice(k * BLOCK, (k + 1) * BLOCK)
            first = b * SLOTS + k * BLOCK
            valid = iota((BLOCK, 1), 0) + first < total
            sent = jnp.concatenate(
                [rows_buf[pl.ds(k * BLOCK * 4 + c, BLOCK, stride=4)] for c in range(4)], axis=1
            ).astype(BF16)
            pre = pre_buf[here] + dot(sent, w_sender[...])
            hidden = silu(pre).astype(BF16)
            update = layer_norm(dot(hidden, w2[...]) + b2_ref[...], gain_ref[...], shift_ref[...])
            update = jnp.where(valid, update, 0.0)
            new = jnp.where(valid, edges_buf[here].astype(F32) + update, 0.0)
            new_far[pl.ds(pl.multiple_of(first, BLOCK), BLOCK)] = new.astype(BF16)
            hot = (iota((NODE, BLOCK), 0) == rcv_ref[b * (SLOTS // BLOCK) + k]).astype(BF16)
            agg[...] += dot(hot, update.astype(BF16))
        return carry

    lax.fori_loop(0, (total + SLOTS - 1) // SLOTS, block, 0)

    stores = []
    for t in range(TILES):
        base = info_ref[t]
        end = info_ref[t + 1]
        first = base // BLOCK
        last = jnp.where(end > base, (end - 1) // BLOCK + 1, first)
        rows = pl.ds(t * TILE, TILE)
        slots = jnp.concatenate([slot_ref[t]] * 8, axis=0).astype(F32)
        slots = jnp.transpose(slots, (1, 0)).astype(jnp.int32)[:, 0:1]
        near[rows] = near_refs[t][...]

        def scatter(b, carry):
            hot = (iota((TILE, BLOCK), 1) + b * BLOCK == slots).astype(BF16)
            there = pl.ds(pl.multiple_of(b * BLOCK, BLOCK), BLOCK)
            near[rows] = near[rows] + dot(hot, new_far[there]).astype(BF16)
            return carry

        lax.fori_loop(first, last, scatter, 0)
        stores.append(pltpu.make_async_copy(near.at[rows], new_edges_ref.at[rows], near_sems.at[1, t]))
        stores[-1].start()

    inner = silu(inner_self + dot(agg[...].astype(BF16), w_aggr[...])).astype(BF16)
    out = layer_norm(dot(inner, wn2[...]) + bn2_ref[...], gain_n_ref[...], shift_n_ref[...])
    new_nodes_ref[...] = nodes_ref[...] + out
    for copy in stores:
        copy.wait()


def full(shape):
    return pl.BlockSpec(shape, lambda *_: (0,) * len(shape))


ANY = pl.BlockSpec(memory_space=pl.ANY)
SMEM = pl.BlockSpec(memory_space=pltpu.SMEM)
VMEM = pl.BlockSpec(memory_space=pltpu.VMEM)
HBM = pl.BlockSpec(memory_space=pltpu.HBM)
ROW = pl.BlockSpec((1, 1, TILE), lambda t: (t, 0, 0))
EDGES = pl.BlockSpec((TILE, D), lambda t: (t, 0))
SQUARE = full((D, D))
VECTOR = full((1, D))


def kept(dims, kind):
    return pltpu.VMEM(dims, kind)


def keep(array):
    return pltpu.with_memory_space_constraint(array, pltpu.VMEM)


def far_away(array):
    return pltpu.with_memory_space_constraint(array, pltpu.HBM)


def shape(dims, kind):
    return jax.ShapeDtypeStruct(dims, kind)


def load_kernel(*refs):
    count = (len(refs) - 1) // 2
    copies = [pltpu.make_async_copy(refs[k], refs[count + k], refs[-1].at[k]) for k in range(count)]
    for copy in copies:
        copy.start()
    for copy in copies:
        copy.wait()


def load(*arrays):
    count = len(arrays)
    return pl.pallas_call(
        load_kernel,
        in_specs=[HBM] * count,
        out_specs=[VMEM] * count,
        out_shape=[kept(array.shape, array.dtype) for array in arrays],
        scratch_shapes=[pltpu.SemaphoreType.DMA((count,))],
        compiler_params=pltpu.CompilerParams(vmem_limit_bytes=16 << 20),
        cost_estimate=pl.CostEstimate(flops=0, bytes_accessed=16 << 20, transcendentals=0),
    )(*(far_away(array) for array in arrays))


def pick(spot, nodes, send_rows):
    return pl.pallas_call(
        pick_kernel,
        in_specs=[SMEM, VMEM, VMEM],
        out_specs=[VMEM] * 5,
        out_shape=(kept((NODE, D), BF16),) + (shape((HALO, D), BF16),) * 4,
        compiler_params=pltpu.CompilerParams(vmem_limit_bytes=16 << 20),
        cost_estimate=pl.CostEstimate(flops=2 * NODE * D * 256, bytes_accessed=2 << 20, transcendentals=0),
    )(spot, nodes, send_rows)


def compact(*args):
    rows = BLOCKS * BLOCK
    return pl.pallas_call(
        compact_kernel,
        in_specs=[SMEM] + [VMEM] * (len(args) - 1),
        out_specs=[VMEM, SMEM, VMEM, VMEM, VMEM, VMEM, ANY, ANY],
        out_shape=(
            kept((TILES, 1, TILE), jnp.int32), shape((16,), jnp.int32),
            shape((BLOCKS, 1, BLOCK), jnp.int32), kept((BLOCKS, 1, BLOCK), jnp.int32),
            kept((NODE, D), BF16), kept((NODE, D), BF16),
            shape((rows, D), BF16), shape((rows, D), F32),
        ),
        scratch_shapes=[
            pltpu.VMEM((TILE, TILE), BF16), pltpu.VMEM((rows, D), BF16),
            pltpu.VMEM((BLOCKS, 8, BLOCK), F32), pltpu.VMEM((rows, D), F32),
            pltpu.SMEM((1,), jnp.int32), pltpu.SemaphoreType.DMA((BLOCKS, 2)),
        ],
        compiler_params=pltpu.CompilerParams(vmem_limit_bytes=30 << 20),
        cost_estimate=pl.CostEstimate(flops=4 << 30, bytes_accessed=8 << 20, transcendentals=0),
    )(*args)


def near(part, pieces, *args):
    outs = [kept((TILE, D), BF16), kept((NODE, D), F32)]
    if part == 0:
        outs = [kept((NEAR, D), BF16)] + outs
    scratch = [pltpu.VMEM((256, D), BF16)]
    if pieces:
        outs = outs + [kept((8192, 4, 128), BF16)]
        scratch = scratch + [pltpu.SemaphoreType.DMA((pieces,))]
    return pl.pallas_call(
        functools.partial(near_kernel, part, pieces),
        in_specs=[SMEM if k == 10 and part == 0 else VMEM for k in range(len(args))],
        out_specs=[VMEM] * len(outs),
        out_shape=outs,
        scratch_shapes=scratch,
        compiler_params=pltpu.CompilerParams(vmem_limit_bytes=16 << 20),
        cost_estimate=pl.CostEstimate(flops=(14 << 30) // PARTS, bytes_accessed=(10 << 20) // PARTS, transcendentals=0),
    )(*args)


def far(*args):
    return pl.pallas_call(
        far_kernel,
        in_specs=[SMEM] * 2 + [VMEM] + [ANY] * LATE + [VMEM] * TILES + [ANY] * 2
        + [VMEM] * (len(args) - 5 - LATE - TILES),
        out_specs=[VMEM, ANY, VMEM],
        out_shape=(shape((NODE, D), F32), shape((EDGE, D), BF16), kept((8192, 4, 128), BF16)),
        input_output_aliases={2: 2},
        scratch_shapes=[
            pltpu.VMEM((4 * SLOTS, 128), F32),
            pltpu.VMEM((SLOTS, D), BF16), pltpu.VMEM((SLOTS, D), F32), pltpu.VMEM((BLOCKS * BLOCK, D), BF16),
            pltpu.VMEM((NODE, D), F32), pltpu.VMEM((EDGE, D), BF16),
            pltpu.SemaphoreType.DMA((LATE,)), pltpu.SemaphoreType.DMA((2, TILES)), pltpu.SemaphoreType.DMA((2,)),
        ],
        compiler_params=pltpu.CompilerParams(vmem_limit_bytes=28 << 20),
        cost_estimate=pl.CostEstimate(flops=4 << 30, bytes_accessed=24 << 20, transcendentals=1 << 20),
    )(*args)


def body(
    nodes, edges, sender, receiver, send_rows,
    w_sender, w_receiver, w_edge, bias_edge1, w_edge2, bias_edge2, gain_edge, shift_edge,
    w_node_self, w_node_aggr, bias_node1, w_node2, bias_node2, gain_node, shift_node,
):
    row = lambda v: v.reshape(1, D)
    tiles = lambda v: v.reshape(TILES, 1, TILE)
    after = lambda v, *first: lax.optimization_barrier((v,) + first)[0]
    x, c, y, z = (lax.axis_index(a) for a in AXES)
    spot = jnp.stack([x, y, z, c]).astype(jnp.int32)
    snd, rcv = tiles(sender), tiles(receiver)
    held = nodes[:COARSE_DEV].astype(BF16).reshape(COARSE_DEV, 4, 128)
    nodes = keep(nodes)
    own, *out = pick(spot, nodes, send_rows)
    own = keep(own)
    tables = jnp.asarray(np.repeat(PLACES.reshape(2, 1, 256), 8, axis=1), BF16)
    place = jnp.where(c == 0, tables[0], tables[1])

    def grow(held, stage, *first):
        got = [from_chip(held, pair) for pair in stage]
        return jnp.concatenate([after(held, *first)] + got, axis=0)

    across = [next_chip(out[2]), other_core(out[3])]
    held = after(grow(held, STAGES[0]), *across)
    halo = [shift_patch(after(out[0], held), 1), shift_patch(after(out[1], held), -1)] + across
    names = load(
        after(edges, held), snd, rcv, w_sender, w_edge, w_edge2, w_receiver,
        w_node_self, w_node_aggr, w_node2,
        row(bias_edge1), row(bias_edge2), row(gain_edge), row(shift_edge),
        row(bias_node1), row(bias_node2), row(gain_node), row(shift_node),
    )
    (
        edges, snd, rcv, w_sender, w_edge, w_edge2, w_receiver, w_node_self, w_node_aggr, w_node2,
        bias_edge1, *vectors,
    ) = (keep(v) for v in names)
    edge_vectors, node_vectors = vectors[:3], vectors[3:]

    def edge_part(part, pieces, *extra):
        return near(part, pieces, snd, rcv, edges, tr, w_edge, bias_edge1, w_edge2, *edge_vectors, *extra)

    held = after(grow(held, STAGES[1]), edges, *halo)
    slot, info, far_code, far_rcv, own_ts, tr, far_edges, far_pre = compact(
        spot, snd, rcv, edges, keep(after(own, held)), w_sender, w_receiver, w_edge, bias_edge1, place,
    )
    slot, far_rcv, own_ts, tr = (keep(v) for v in (slot, far_rcv, own_ts, tr))
    held = grow(held, STAGES[2], tr)
    last = [from_chip(held, pair) for pair in LAST]
    ts, edges_0, agg = edge_part(0, 0, spot, keep(after(own_ts, held)), *halo, w_sender)
    ts, edges_0, agg = keep(ts), keep(edges_0), keep(agg)
    edges_1, agg = (keep(v) for v in edge_part(1, 0, ts, agg))
    first = [other_core(held), other_core(after(last[0], agg))]
    edges_2, agg = (keep(v) for v in edge_part(2, 0, ts, agg))
    second = [other_core(after(piece, agg)) for piece in last[1:]]
    early = [held, *last, *first]
    edges_3, agg, table = (keep(v) for v in edge_part(3, 6, ts, agg, *early))
    new_nodes, new_edges, _ = far(
        info, far_code, table, *second, edges_0, edges_1, edges_2, edges_3,
        far_edges, far_pre, agg, slot, far_rcv, nodes,
        w_sender, w_edge2, w_node_self, w_node_aggr, w_node2, *edge_vectors, *node_vectors,
    )
    return new_nodes, new_edges


def solution(mesh):
    grid = Mesh(mesh.devices.reshape(SIZES), AXES)
    split = P(AXES, None)
    return jax.shard_map(
        body,
        mesh=grid,
        in_specs=(split, split, P(AXES), P(AXES), split) + (P(),) * 15,
        out_specs=(split, split),
        check_vma=False,
    )
```

```python
import functools

import numpy as np
import jax
import jax.numpy as jnp
from jax import lax
from jax.experimental import pallas as pl
from jax.experimental.pallas import tpu as pltpu
from jax.sharding import Mesh, PartitionSpec as P

AXES = ("x", "core", "y", "z")
SIZES = (4, 2, 4, 8)
NODE = 512
HALO = 64
NEAR = NODE + 4 * HALO
COARSE_DEV = 32
D = 512
EDGE = 4096
TILE = 1024
TILES = EDGE // TILE
BLOCK = 256
SLOTS = 768
BLOCKS = 18
LATE = 2
WINDOW = 240
SUB = 512
F32 = jnp.float32
BF16 = jnp.bfloat16

STAGES = (
    (((0, 0, 4),) * 2,),
    (((2, 0, 0), (0, 2, 0)), ((0, 2, 0), (2, 0, 0)), ((2, 2, 0),) * 2),
    (((1, 1, 1), (-1, -1, -1)), ((-1, -1, -1), (1, 1, 1)), ((0, 0, 2), (0, 0, -2))),
)
LAST = (((1, 0, 0), (-1, 0, 0)), ((0, 1, 0), (0, -1, 0)), ((0, 0, 1), (0, 0, -1)))


def places():
    own = np.zeros((2, 128), np.int32)
    for core in range(2):
        held = [(0, 0, 0)]
        for stage in STAGES + (LAST,):
            held = [
                ((a[0] + o[0]) % 4, (a[1] + o[1]) % 4, (a[2] + o[2]) % 8)
                for o in [(0, 0, 0)] + [pair[core] for pair in stage]
                for a in held
            ]
        assert len(set(held)) == 128
        for block, (x, y, z) in enumerate(held):
            own[core, x * 32 + y * 8 + z] = block
    return np.stack([np.stack([own[c] if c == k else 128 + own[k] for k in range(2)]) for c in range(2)])


PLACES = places()


def device(x, c, y, z):
    return ((x % 4) * 2 + c % 2) * 32 + (y % 4) * 8 + z % 8


def receive(block, source):
    spots = [(x, c, y, z) for x in range(4) for c in range(2) for y in range(4) for z in range(8)]
    return lax.ppermute(block, AXES, [(device(*source(*spot)), device(*spot)) for spot in spots])


def from_chip(block, pair):
    return receive(block, lambda x, c, y, z: (x + pair[c][0], c, y + pair[c][1], z + pair[c][2]))


def other_core(block):
    return receive(block, lambda x, c, y, z: (x, 1 - c, y, z))


def shift_patch(block, step):
    def source(x, c, y, z):
        j = (y * 8 + z - step) % 32
        return x, c, j // 8, j % 8

    return receive(block, source)


def next_chip(block):
    return receive(block, lambda x, c, y, z: (x - 1 + 2 * c, 1 - c, y, z))


def dot(a, b):
    return jnp.dot(a, b, preferred_element_type=F32)


def dot_first(a, b):
    return lax.dot_general(a, b, (((0,), (0,)), ((), ())), preferred_element_type=F32)


def dot_last(a, b):
    return lax.dot_general(a, b, (((1,), (1,)), ((), ())), preferred_element_type=F32)


def silu(v):
    half = 0.5 * v
    return half + half * jnp.tanh(half)


def layer_norm(v, gain, shift):
    center = v - jnp.mean(v, axis=-1, keepdims=True)
    spread = jnp.mean(center * center, axis=-1, keepdims=True)
    return center * lax.rsqrt(spread + 1e-05) * gain + shift


def iota(shape, dim):
    return lax.broadcasted_iota(jnp.int32, shape, dim)


def pick_kernel(spot_ref, nodes_ref, rows_ref, own_ref, *out_refs):
    own = nodes_ref[...].astype(BF16)
    own_ref[...] = own
    core = spot_ref[3]
    for row, out_ref in zip((0, 1, 3 - core, 2 + core), out_refs):
        hot = (iota((NODE, HALO), 0) == rows_ref[pl.ds(row, 1), :]).astype(BF16)
        out_ref[...] = dot_first(hot, own).astype(BF16)


def compact_kernel(
    spot_ref, snd_ref, rcv_ref, edges_ref, own_ref, w_sender_ref, w_receiver_ref, w_edge_ref, b1_ref, place_ref,
    slot_ref, info_ref, code_out_ref, rcv_out_ref, ts_ref, tr_ref, far_edges_ref, far_pre_ref,
    upper, far_edges, far_meta, far_pre, count, sems,
):
    ts_ref[...] = dot(own_ref[...], w_sender_ref[...]).astype(BF16)
    tr_ref[...] = dot(own_ref[...], w_receiver_ref[...]).astype(BF16)
    upper[...] = (iota((TILE, TILE), 0) < iota((TILE, TILE), 1)).astype(BF16)
    rcv_out_ref[...] = jnp.full_like(rcv_out_ref, NODE)
    count[0] = 0

    def tile(t, carry):
        compact_tile(
            t, spot_ref, snd_ref, rcv_ref, edges_ref, slot_ref, info_ref, upper, far_edges, far_meta, count,
        )
        return carry

    lax.fori_loop(0, TILES, tile, 0)
    total = count[0]
    info_ref[TILES] = total
    blocks = (total + BLOCK - 1) // BLOCK

    def copies(b):
        rows = pl.ds(pl.multiple_of(b * BLOCK, BLOCK), BLOCK)
        return (
            pltpu.make_async_copy(far_edges.at[rows], far_edges_ref.at[rows], sems.at[b, 0]),
            pltpu.make_async_copy(far_pre.at[rows], far_pre_ref.at[rows], sems.at[b, 1]),
        )

    def push(b, carry):
        info = far_meta[b].astype(jnp.int32)
        spots = (iota((256, BLOCK), 0) == info[0:1]).astype(BF16)
        block = dot(place_ref[...], spots)[0:1].astype(jnp.int32)
        code_out_ref[b] = block * 32 + info[1:2]
        live = iota((1, BLOCK), 1) + b * BLOCK < total
        rcv_b = jnp.where(live, info[2:3] * 128 + info[3:4], NODE)
        rcv_out_ref[b] = rcv_b
        rows = pl.ds(pl.multiple_of(b * BLOCK, BLOCK), BLOCK)
        hot = (iota((NODE, BLOCK), 0) == jnp.minimum(rcv_b, NODE - 1)).astype(BF16)
        far_pre[rows] = dot(far_edges[rows], w_edge_ref[...]) + dot_first(hot, tr_ref[...]) + b1_ref[...]
        for copy in copies(b):
            copy.start()
        return carry

    lax.fori_loop(0, blocks, push, 0)

    def settle(b, carry):
        for copy in copies(b):
            copy.wait()
        return carry

    lax.fori_loop(0, blocks, settle, 0)


def compact_tile(t, spot_ref, snd_ref, rcv_ref, edges_ref, slot_ref, info_ref, upper, far_edges, far_meta, count):
    rcv = rcv_ref[t]
    snd = snd_ref[t]
    far = snd >= NEAR
    q = jnp.maximum(snd - NEAR, 0)
    p = q >> 5
    dx = ((p >> 6) - spot_ref[0]) & 3
    dy = ((p >> 3) - spot_ref[1]) & 3
    dz = (p - spot_ref[2]) & 7
    place = (((p >> 5) & 1) << 7) | (dx << 5) | (dy << 3) | dz
    far_f = far.astype(F32)
    base = count[0]
    before = dot(jnp.broadcast_to(far_f, (8, TILE)).astype(BF16), upper[...])[0:1].astype(jnp.int32)
    number = jnp.sum(far_f).astype(jnp.int32)
    slot = jnp.where(far, base + before, -1)
    slot_ref[t] = slot
    info_ref[t] = base
    count[0] = base + number
    first = base // BLOCK
    last = jnp.where(number > 0, (base + number - 1) // BLOCK + 1, first)
    zero = jnp.zeros_like(rcv)
    meta = jnp.concatenate([place, q & 31, rcv >> 7, rcv & 127, zero, zero, zero, zero], axis=0)
    meta = meta.astype(F32).astype(BF16)

    def gather(b, carry):
        hot = (iota((BLOCK, TILE), 0) + b * BLOCK == slot).astype(BF16)
        rows = pl.ds(pl.multiple_of(b * BLOCK, BLOCK), BLOCK)
        fresh = b * BLOCK >= base
        far_edges[rows] = jnp.where(fresh, 0.0, far_edges[rows]) + dot(hot, edges_ref[pl.ds(pl.multiple_of(t * TILE, TILE), TILE)]).astype(BF16)
        far_meta[b] = jnp.where(fresh, 0.0, far_meta[b]) + dot_last(meta, hot)
        return carry

    lax.fori_loop(first, last, gather, 0)


def near_kernel(begin, end, pieces, *refs):
    (
        snd_ref, rcv_ref, edges_ref, tr_ref,
        w_edge_ref, b1_ref, w2_ref, b2_ref, gain_ref, shift_ref,
    ) = refs[:10]
    window, snd_c, rcv_c, updates = refs[-4:]
    if begin == 0:
        spot_ref, own_ts_ref, h0_ref, h1_ref, h2_ref, h3_ref, w_sender_ref = refs[10:17]
        new_edges_ref, agg_ref, ts_ref = refs[17:20]
        w_sender = w_sender_ref[...]
        ts_ref[:NODE] = own_ts_ref[...]
        core = spot_ref[3]
        for k, h_ref in zip((0, 1, 2 + core, 3 - core), (h0_ref, h1_ref, h2_ref, h3_ref)):
            there = pl.ds(pl.multiple_of(NODE + k * HALO, HALO), HALO)
            ts_ref[there] = dot(h_ref[...], w_sender).astype(BF16)
        agg_ref[...] = jnp.zeros_like(agg_ref)
    else:
        ts_ref = refs[10]
        ready = refs[13:13 + pieces]
        new_edges_ref, agg_ref = refs[13 + pieces:15 + pieces]
        if pieces:
            table, sems = refs[15 + pieces:17 + pieces]
        copies = [
            pltpu.make_async_copy(piece, table.at[k * 1024:(k + 1) * 1024], sems.at[k])
            for k, piece in enumerate(ready)
        ]
        for copy in copies:
            copy.start()
    window[WINDOW:] = tr_ref[NODE - 16:]

    def edge_rows(at, col, hots, tables):
        edges = edges_ref[at]
        pre = dot(edges, w_edge_ref[...]) + b1_ref[...]
        for hot, part in zip(hots, tables):
            pre = pre + dot(hot, part)
        hidden = silu(pre).astype(BF16)
        update = layer_norm(dot(hidden, w2_ref[...]) + b2_ref[...], gain_ref[...], shift_ref[...])
        new_edges_ref[at] = jnp.where(col >= 0, edges.astype(F32) + update, 0.0).astype(BF16)
        return update.astype(BF16)

    def columns(*rows):
        both = jnp.concatenate(list(rows) * 4, axis=0)
        cols = jnp.transpose(both.astype(F32), (1, 0)).astype(jnp.int32)
        return cols[:, 0:1], cols[:, 1:2]

    def step(i, carry):
        snd = snd_ref[i]
        rcv = rcv_ref[i]
        far = snd >= NEAR
        live = rcv < NODE
        low = jnp.min(rcv)
        high = jnp.max(jnp.where(live, rcv, -1))
        start = pl.multiple_of(jnp.minimum(low // 16 * 16, NODE - WINDOW), 16)
        narrow = high - start < WINDOW
        snd_n = jnp.where(far, -1, snd)

        @pl.when(narrow)
        def _():
            window[:WINDOW] = tr_ref[pl.ds(start, WINDOW)]
            snd_v, rcv_v = columns(snd_n, jnp.where(live, rcv - start, WINDOW + 15))
            parts = []
            for k in range(0, TILE, SUB):
                col = snd_v[k:k + SUB]
                hot_s = (iota((SUB, NEAR), 1) == col).astype(BF16)
                hot_r = (iota((SUB, 256), 1) == rcv_v[k:k + SUB]).astype(BF16)
                at = pl.ds(pl.multiple_of(i * TILE + k, SUB), SUB)
                parts.append(edge_rows(at, col, [hot_s, hot_r], [ts_ref[...], window[...]]))
            hot_n = (iota((WINDOW, TILE), 0) == jnp.where(far, -1, rcv - start)).astype(BF16)
            agg_ref[pl.ds(start, WINDOW)] += dot(hot_n, jnp.concatenate(parts, axis=0))

        @pl.when(jnp.logical_not(narrow))
        def _():
            snd_v, rcv_v = columns(snd_n, jnp.minimum(rcv, NODE - 1))
            snd_c[...] = snd_v
            rcv_c[...] = rcv_v

            def some(j, c):
                at = pl.ds(pl.multiple_of(j * 128, 128), 128)
                col = snd_c[at]
                hot_s = (iota((128, NEAR), 1) == col).astype(BF16)
                hot_r = (iota((128, NODE), 1) == rcv_c[at]).astype(BF16)
                there = pl.ds(pl.multiple_of(i * TILE + j * 128, 128), 128)
                updates[at] = edge_rows(there, col, [hot_s, hot_r], [ts_ref[...], tr_ref[...]])
                return c

            lax.fori_loop(0, TILE // 128, some, 0)

            def sums(j, c):
                at = pl.ds(pl.multiple_of(j * 128, 128), 128)
                hot_n = (iota((128, TILE), 0) + j * 128 == jnp.where(far, -1, rcv)).astype(BF16)
                agg_ref[at] += dot(hot_n, updates[...])
                return c

            lax.fori_loop(0, NODE // 128, sums, 0)

        return carry

    lax.fori_loop(begin, end, step, 0)
    if begin and pieces:
        for copy in copies:
            copy.wait()


def far_kernel(info_ref, code_ref, *refs):
    late = refs[1:1 + LATE]
    (
        _, far_edges_ref, far_pre_ref, agg_ref, slot_ref, rcv_ref, nodes_ref,
        w_sender, w2, w_self, w_aggr, wn2,
        b2_ref, gain_ref, shift_ref, bn1_ref, bn2_ref, gain_n_ref, shift_n_ref,
        new_nodes_ref, new_edges_ref, table, near,
        rows_buf, edges_buf, pre_buf, new_far, agg, sems, near_sems, row_sems,
    ) = refs[1 + LATE:]
    copies = [
        pltpu.make_async_copy(piece, table.at[(8 - LATE + k) * 1024:(9 - LATE + k) * 1024], sems.at[k])
        for k, piece in enumerate(late)
    ]

    def block_copies(b):
        rows = pl.ds(pl.multiple_of(b * SLOTS, SLOTS), SLOTS)
        return (
            pltpu.make_async_copy(far_edges_ref.at[rows], edges_buf, row_sems.at[0]),
            pltpu.make_async_copy(far_pre_ref.at[rows], pre_buf, row_sems.at[1]),
        )

    total = info_ref[TILES]
    for copy in copies:
        copy.start()

    @pl.when(total > 0)
    def _():
        for copy in block_copies(0):
            copy.start()

    agg[...] = agg_ref[...]
    inner_self = dot(nodes_ref[...].astype(BF16), w_self[...]) + bn1_ref[...]
    for copy in copies:
        copy.wait()

    def block(b, carry):
        @pl.when(b > 0)
        def _():
            for copy in block_copies(b):
                copy.start()

        count = jnp.minimum(SLOTS, (total - b * SLOTS + 15) // 16 * 16)

        row = b * (SLOTS // BLOCK)

        def gather(i, c):
            for k in range(16):
                slot = i * 16 + k
                code = code_ref[row + (slot >> 8), 0, slot & 255]
                rows_buf[pl.ds(pl.multiple_of(slot * 4, 4), 4)] = table[code].astype(F32)
            return c

        lax.fori_loop(0, count // 16, gather, 0)
        for copy in block_copies(b):
            copy.wait()
        for k in range(SLOTS // BLOCK):
            here = slice(k * BLOCK, (k + 1) * BLOCK)
            first = b * SLOTS + k * BLOCK
            valid = iota((BLOCK, 1), 0) + first < total
            sent = jnp.concatenate(
                [rows_buf[pl.ds(k * BLOCK * 4 + c, BLOCK, stride=4)] for c in range(4)], axis=1
            ).astype(BF16)
            pre = pre_buf[here] + dot(sent, w_sender[...])
            hidden = silu(pre).astype(BF16)
            update = layer_norm(dot(hidden, w2[...]) + b2_ref[...], gain_ref[...], shift_ref[...])
            update = jnp.where(valid, update, 0.0)
            new = jnp.where(valid, edges_buf[here].astype(F32) + update, 0.0)
            new_far[pl.ds(pl.multiple_of(first, BLOCK), BLOCK)] = new.astype(BF16)
            hot = (iota((NODE, BLOCK), 0) == rcv_ref[b * (SLOTS // BLOCK) + k]).astype(BF16)
            agg[...] += dot(hot, update.astype(BF16))
        return carry

    lax.fori_loop(0, (total + SLOTS - 1) // SLOTS, block, 0)

    def store(t):
        rows = pl.ds(pl.multiple_of(t * TILE, TILE), TILE)
        return pltpu.make_async_copy(near.at[rows], new_edges_ref.at[rows], near_sems.at[t])

    def tile(t, carry):
        base = info_ref[t]
        end = info_ref[t + 1]
        first = base // BLOCK
        last = jnp.where(end > base, (end - 1) // BLOCK + 1, first)
        rows = pl.ds(pl.multiple_of(t * TILE, TILE), TILE)
        slots = jnp.concatenate([slot_ref[t]] * 8, axis=0).astype(F32)
        slots = jnp.transpose(slots, (1, 0)).astype(jnp.int32)[:, 0:1]

        def scatter(b, c):
            hot = (iota((TILE, BLOCK), 1) + b * BLOCK == slots).astype(BF16)
            there = pl.ds(pl.multiple_of(b * BLOCK, BLOCK), BLOCK)
            near[rows] = near[rows] + dot(hot, new_far[there]).astype(BF16)
            return c

        lax.fori_loop(first, last, scatter, 0)
        store(t).start()
        return carry

    lax.fori_loop(0, TILES, tile, 0)
    inner = silu(inner_self + dot(agg[...].astype(BF16), w_aggr[...])).astype(BF16)
    out = layer_norm(dot(inner, wn2[...]) + bn2_ref[...], gain_n_ref[...], shift_n_ref[...])
    new_nodes_ref[...] = nodes_ref[...] + out
    for t in range(TILES):
        store(t).wait()


def full(shape):
    return pl.BlockSpec(shape, lambda *_: (0,) * len(shape))


ANY = pl.BlockSpec(memory_space=pl.ANY)
SMEM = pl.BlockSpec(memory_space=pltpu.SMEM)
VMEM = pl.BlockSpec(memory_space=pltpu.VMEM)
HBM = pl.BlockSpec(memory_space=pltpu.HBM)
ROW = pl.BlockSpec((1, 1, TILE), lambda t: (t, 0, 0))
EDGES = pl.BlockSpec((TILE, D), lambda t: (t, 0))
SQUARE = full((D, D))
VECTOR = full((1, D))


def kept(dims, kind):
    return pltpu.VMEM(dims, kind)


def keep(array):
    return pltpu.with_memory_space_constraint(array, pltpu.VMEM)


def far_away(array):
    return pltpu.with_memory_space_constraint(array, pltpu.HBM)


def shape(dims, kind):
    return jax.ShapeDtypeStruct(dims, kind)


def load_kernel(*refs):
    count = (len(refs) - 1) // 2
    copies = [pltpu.make_async_copy(refs[k], refs[count + k], refs[-1].at[k]) for k in range(count)]
    for copy in copies:
        copy.start()
    for copy in copies:
        copy.wait()


def load(*arrays):
    count = len(arrays)
    return pl.pallas_call(
        load_kernel,
        in_specs=[HBM] * count,
        out_specs=[VMEM] * count,
        out_shape=[kept(array.shape, array.dtype) for array in arrays],
        scratch_shapes=[pltpu.SemaphoreType.DMA((count,))],
        compiler_params=pltpu.CompilerParams(vmem_limit_bytes=16 << 20),
        cost_estimate=pl.CostEstimate(flops=0, bytes_accessed=16 << 20, transcendentals=0),
    )(*(far_away(array) for array in arrays))


def pick(spot, nodes, send_rows):
    return pl.pallas_call(
        pick_kernel,
        in_specs=[SMEM, VMEM, VMEM],
        out_specs=[VMEM] * 5,
        out_shape=(kept((NODE, D), BF16),) + (shape((HALO, D), BF16),) * 4,
        compiler_params=pltpu.CompilerParams(vmem_limit_bytes=16 << 20),
        cost_estimate=pl.CostEstimate(flops=2 * NODE * D * 256, bytes_accessed=2 << 20, transcendentals=0),
    )(spot, nodes, send_rows)


def compact(*args):
    rows = BLOCKS * BLOCK
    return pl.pallas_call(
        compact_kernel,
        in_specs=[SMEM] + [VMEM] * (len(args) - 1),
        out_specs=[VMEM, SMEM, VMEM, VMEM, VMEM, VMEM, HBM, HBM],
        out_shape=(
            kept((TILES, 1, TILE), jnp.int32), shape((16,), jnp.int32),
            shape((BLOCKS, 1, BLOCK), jnp.int32), kept((BLOCKS, 1, BLOCK), jnp.int32),
            kept((NODE, D), BF16), kept((NODE, D), BF16),
            pltpu.HBM((rows, D), BF16), pltpu.HBM((rows, D), F32),
        ),
        scratch_shapes=[
            pltpu.VMEM((TILE, TILE), BF16), pltpu.VMEM((rows, D), BF16),
            pltpu.VMEM((BLOCKS, 8, BLOCK), F32), pltpu.VMEM((rows, D), F32),
            pltpu.SMEM((1,), jnp.int32), pltpu.SemaphoreType.DMA((BLOCKS, 2)),
        ],
        compiler_params=pltpu.CompilerParams(vmem_limit_bytes=30 << 20),
        cost_estimate=pl.CostEstimate(flops=4 << 30, bytes_accessed=8 << 20, transcendentals=0),
    )(*args)


def near(begin, end, pieces, *args):
    outs = [kept((EDGE, D), BF16), kept((NODE, D), F32)]
    scratch = [
        pltpu.VMEM((256, D), BF16), pltpu.VMEM((TILE, 1), jnp.int32), pltpu.VMEM((TILE, 1), jnp.int32),
        pltpu.VMEM((TILE, D), BF16),
    ]
    if begin == 0:
        outs = outs + [kept((NEAR, D), BF16)]
    if pieces:
        outs = outs + [kept((8192, 4, 128), BF16)]
        scratch = [pltpu.SemaphoreType.DMA((pieces,))] + scratch
    return pl.pallas_call(
        functools.partial(near_kernel, begin, end, pieces),
        in_specs=[SMEM if k == 10 and begin == 0 else VMEM for k in range(len(args))],
        out_specs=[VMEM] * len(outs),
        out_shape=outs,
        scratch_shapes=scratch,
        input_output_aliases={11: 0, 12: 1} if begin else {},
        compiler_params=pltpu.CompilerParams(vmem_limit_bytes=16 << 20),
        cost_estimate=pl.CostEstimate(flops=(end - begin) << 31, bytes_accessed=(end - begin) << 21, transcendentals=0),
    )(*args)


def far(*args):
    return pl.pallas_call(
        far_kernel,
        in_specs=[SMEM] * 2 + [VMEM] + [ANY] * LATE + [VMEM] + [HBM] * 2 + [VMEM] * (len(args) - 6 - LATE),
        out_specs=[VMEM, ANY, VMEM, VMEM],
        out_shape=(shape((NODE, D), F32), shape((EDGE, D), BF16), kept((8192, 4, 128), BF16), kept((EDGE, D), BF16)),
        input_output_aliases={2: 2, 3 + LATE: 3},
        scratch_shapes=[
            pltpu.VMEM((4 * SLOTS, 128), F32),
            pltpu.VMEM((SLOTS, D), BF16), pltpu.VMEM((SLOTS, D), F32), pltpu.VMEM((BLOCKS * BLOCK, D), BF16),
            pltpu.VMEM((NODE, D), F32),
            pltpu.SemaphoreType.DMA((LATE,)), pltpu.SemaphoreType.DMA((TILES,)), pltpu.SemaphoreType.DMA((2,)),
        ],
        compiler_params=pltpu.CompilerParams(vmem_limit_bytes=24 << 20),
        cost_estimate=pl.CostEstimate(flops=4 << 30, bytes_accessed=24 << 20, transcendentals=1 << 20),
    )(*args)


def body(
    nodes, edges, sender, receiver, send_rows,
    w_sender, w_receiver, w_edge, bias_edge1, w_edge2, bias_edge2, gain_edge, shift_edge,
    w_node_self, w_node_aggr, bias_node1, w_node2, bias_node2, gain_node, shift_node,
):
    row = lambda v: v.reshape(1, D)
    tiles = lambda v: v.reshape(TILES, 1, TILE)
    after = lambda v, *first: lax.optimization_barrier((v,) + first)[0]
    x, c, y, z = (lax.axis_index(a) for a in AXES)
    spot = jnp.stack([x, y, z, c]).astype(jnp.int32)
    held = nodes[:COARSE_DEV].astype(BF16).reshape(COARSE_DEV, 4, 128)
    nodes = keep(nodes)
    own, *out = pick(spot, nodes, send_rows)
    own = keep(own)
    tables = jnp.asarray(np.repeat(PLACES.reshape(2, 1, 256), 8, axis=1), BF16)
    place = jnp.where(c == 0, tables[0], tables[1])

    def grow(held, stage, *first):
        got = [from_chip(held, pair) for pair in stage]
        return jnp.concatenate([after(held, *first)] + got, axis=0)

    across = [next_chip(out[2]), other_core(out[3])]
    held = after(grow(held, STAGES[0]), *across)
    halo = [shift_patch(after(out[0], held), 1), shift_patch(after(out[1], held), -1)] + across
    names = load(
        after(edges, held), tiles(sender), tiles(receiver), w_sender, w_edge, w_edge2, w_receiver,
        w_node_self, w_node_aggr, w_node2,
        row(bias_edge1), row(bias_edge2), row(gain_edge), row(shift_edge),
        row(bias_node1), row(bias_node2), row(gain_node), row(shift_node),
    )
    (
        edges, snd, rcv, w_sender, w_edge, w_edge2, w_receiver, w_node_self, w_node_aggr, w_node2,
        bias_edge1, *vectors,
    ) = (keep(v) for v in names)
    edge_vectors, node_vectors = vectors[:3], vectors[3:]

    def edge_part(begin, end, pieces, *extra):
        outs = near(begin, end, pieces, snd, rcv, edges, tr, w_edge, bias_edge1, w_edge2, *edge_vectors, *extra)
        return [keep(v) for v in outs]

    held = after(grow(held, STAGES[1]), edges, *halo)
    slot, info, far_code, far_rcv, own_ts, tr, far_edges, far_pre = compact(
        spot, snd, rcv, edges, keep(after(own, held)), w_sender, w_receiver, w_edge, bias_edge1, place,
    )
    slot, far_rcv, own_ts, tr = (keep(v) for v in (slot, far_rcv, own_ts, tr))
    held = grow(held, STAGES[2], tr)
    last = [from_chip(held, pair) for pair in LAST]
    done, agg, ts = edge_part(0, 2, 0, spot, keep(after(own_ts, held)), *halo, w_sender)
    first = [other_core(held), other_core(after(last[0], agg))]
    done, agg = edge_part(2, 3, 0, ts, done, agg)
    second = [other_core(after(piece, agg)) for piece in last[1:]]
    early = [held, *last, *first]
    done, agg, table = edge_part(3, 4, 6, ts, done, agg, *early)
    new_nodes, new_edges, _, _ = far(
        info, far_code, table, *second, done,
        far_away(far_edges), far_away(far_pre), agg, slot, far_rcv, nodes,
        w_sender, w_edge2, w_node_self, w_node_aggr, w_node2, *edge_vectors, *node_vectors,
    )
    return new_nodes, new_edges


def solution(mesh):
    grid = Mesh(mesh.devices.reshape(SIZES), AXES)
    split = P(AXES, None)
    return jax.shard_map(
        body,
        mesh=grid,
        in_specs=(split, split, P(AXES), P(AXES), split) + (P(),) * 15,
        out_specs=(split, split),
        check_vma=False,
    )
```

```python
import functools

import numpy as np
import jax
import jax.numpy as jnp
from jax import lax
from jax.experimental import pallas as pl
from jax.experimental.pallas import tpu as pltpu
from jax.sharding import Mesh, PartitionSpec as P

AXES = ("x", "core", "y", "z")
SIZES = (4, 2, 4, 8)
NODE = 512
HALO = 64
NEAR = NODE + 4 * HALO
COARSE_DEV = 32
D = 512
EDGE = 4096
TILE = 1024
TILES = EDGE // TILE
BLOCK = 256
SLOTS = 768
BLOCKS = 18
LATE = 2
WINDOW = 240
SUB = 512
F32 = jnp.float32
BF16 = jnp.bfloat16

STAGES = (
    (((0, 0, 4),) * 2,),
    (((2, 0, 0), (0, 2, 0)), ((0, 2, 0), (2, 0, 0)), ((2, 2, 0),) * 2),
    (((1, 1, 1), (-1, -1, -1)), ((-1, -1, -1), (1, 1, 1)), ((0, 0, 2), (0, 0, -2))),
)
LAST = (((1, 0, 0), (-1, 0, 0)), ((0, 1, 0), (0, -1, 0)), ((0, 0, 1), (0, 0, -1)))


def places():
    own = np.zeros((2, 128), np.int32)
    for core in range(2):
        held = [(0, 0, 0)]
        for stage in STAGES + (LAST,):
            held = [
                ((a[0] + o[0]) % 4, (a[1] + o[1]) % 4, (a[2] + o[2]) % 8)
                for o in [(0, 0, 0)] + [pair[core] for pair in stage]
                for a in held
            ]
        assert len(set(held)) == 128
        for block, (x, y, z) in enumerate(held):
            own[core, x * 32 + y * 8 + z] = block
    return np.stack([np.stack([own[c] if c == k else 128 + own[k] for k in range(2)]) for c in range(2)])


PLACES = places()


def device(x, c, y, z):
    return ((x % 4) * 2 + c % 2) * 32 + (y % 4) * 8 + z % 8


def receive(block, source):
    spots = [(x, c, y, z) for x in range(4) for c in range(2) for y in range(4) for z in range(8)]
    return lax.ppermute(block, AXES, [(device(*source(*spot)), device(*spot)) for spot in spots])


def from_chip(block, pair):
    return receive(block, lambda x, c, y, z: (x + pair[c][0], c, y + pair[c][1], z + pair[c][2]))


def other_core(block):
    return receive(block, lambda x, c, y, z: (x, 1 - c, y, z))


def shift_patch(block, step):
    def source(x, c, y, z):
        j = (y * 8 + z - step) % 32
        return x, c, j // 8, j % 8

    return receive(block, source)


def next_chip(block):
    return receive(block, lambda x, c, y, z: (x - 1 + 2 * c, 1 - c, y, z))


def dot(a, b):
    return jnp.dot(a, b, preferred_element_type=F32)


def dot_first(a, b):
    return lax.dot_general(a, b, (((0,), (0,)), ((), ())), preferred_element_type=F32)


def dot_last(a, b):
    return lax.dot_general(a, b, (((1,), (1,)), ((), ())), preferred_element_type=F32)


def silu(v):
    half = 0.5 * v
    return half + half * jnp.tanh(half)


def layer_norm(v, gain, shift):
    center = v - jnp.mean(v, axis=-1, keepdims=True)
    spread = jnp.mean(center * center, axis=-1, keepdims=True)
    return center * lax.rsqrt(spread + 1e-05) * gain + shift


def iota(shape, dim):
    return lax.broadcasted_iota(jnp.int32, shape, dim)


def pick_kernel(spot_ref, nodes_in, rows_in, nodes_ref, own_ref, *refs):
    out_refs = refs[:4]
    rows_ref, sems = refs[4:]
    copies = [
        pltpu.make_async_copy(nodes_in, nodes_ref, sems.at[0]), pltpu.make_async_copy(rows_in, rows_ref, sems.at[1]),
    ]
    for copy in copies:
        copy.start()
    for copy in copies:
        copy.wait()
    own = nodes_ref[...].astype(BF16)
    own_ref[...] = own
    core = spot_ref[3]
    for row, out_ref in zip((0, 1, 3 - core, 2 + core), out_refs):
        hot = (iota((NODE, HALO), 0) == rows_ref[pl.ds(row, 1), :]).astype(BF16)
        out_ref[...] = dot_first(hot, own).astype(BF16)


def compact_kernel(
    spot_ref, snd_ref, rcv_ref, edges_ref, own_ref, w_sender_ref, w_receiver_ref, w_edge_ref, b1_ref, place_ref,
    slot_ref, info_ref, code_out_ref, rcv_out_ref, ts_ref, tr_ref, far_edges_ref, far_pre_ref,
    upper, far_edges, far_meta, far_pre, count, sems,
):
    ts_ref[...] = dot(own_ref[...], w_sender_ref[...]).astype(BF16)
    tr_ref[...] = dot(own_ref[...], w_receiver_ref[...]).astype(BF16)
    upper[...] = (iota((256, 256), 0) < iota((256, 256), 1)).astype(BF16)
    rcv_out_ref[...] = jnp.full_like(rcv_out_ref, NODE)
    count[0] = 0

    def tile(t, carry):
        compact_tile(
            t, spot_ref, snd_ref, rcv_ref, edges_ref, slot_ref, info_ref, upper, far_edges, far_meta, count,
        )
        return carry

    lax.fori_loop(0, TILES, tile, 0)
    total = count[0]
    info_ref[TILES] = total
    blocks = (total + BLOCK - 1) // BLOCK

    def copies(b):
        rows = pl.ds(pl.multiple_of(b * BLOCK, BLOCK), BLOCK)
        return (
            pltpu.make_async_copy(far_edges.at[rows], far_edges_ref.at[rows], sems.at[b, 0]),
            pltpu.make_async_copy(far_pre.at[rows], far_pre_ref.at[rows], sems.at[b, 1]),
        )

    def push(b, carry):
        info = far_meta[b].astype(jnp.int32)
        spots = (iota((256, BLOCK), 0) == info[0:1]).astype(BF16)
        block = dot(place_ref[...], spots)[0:1].astype(jnp.int32)
        code_out_ref[b] = block * 32 + info[1:2]
        live = iota((1, BLOCK), 1) + b * BLOCK < total
        rcv_b = jnp.where(live, info[2:3] * 128 + info[3:4], NODE)
        rcv_out_ref[b] = rcv_b
        rows = pl.ds(pl.multiple_of(b * BLOCK, BLOCK), BLOCK)
        hot = (iota((NODE, BLOCK), 0) == jnp.minimum(rcv_b, NODE - 1)).astype(BF16)
        far_pre[rows] = dot(far_edges[rows], w_edge_ref[...]) + dot_first(hot, tr_ref[...]) + b1_ref[...]
        for copy in copies(b):
            copy.start()
        return carry

    lax.fori_loop(0, blocks, push, 0)

    def settle(b, carry):
        for copy in copies(b):
            copy.wait()
        return carry

    lax.fori_loop(0, blocks, settle, 0)


def compact_tile(t, spot_ref, snd_ref, rcv_ref, edges_ref, slot_ref, info_ref, upper, far_edges, far_meta, count):
    rcv = rcv_ref[t]
    snd = snd_ref[t]
    far = snd >= NEAR
    q = jnp.maximum(snd - NEAR, 0)
    p = q >> 5
    dx = ((p >> 6) - spot_ref[0]) & 3
    dy = ((p >> 3) - spot_ref[1]) & 3
    dz = (p - spot_ref[2]) & 7
    place = (((p >> 5) & 1) << 7) | (dx << 5) | (dy << 3) | dz
    far_f = far.astype(F32)
    base = count[0]
    wide = jnp.broadcast_to(far_f, (8, TILE)).astype(BF16)
    before, passed = [], jnp.zeros((1, 1), F32)
    for k in range(0, TILE, 256):
        before.append(dot(wide[:, k:k + 256], upper[...])[0:1] + passed)
        passed = passed + jnp.sum(far_f[:, k:k + 256], axis=1, keepdims=True)
    before = jnp.concatenate(before, axis=1).astype(jnp.int32)
    number = jnp.sum(far_f).astype(jnp.int32)
    slot = jnp.where(far, base + before, -1)
    slot_ref[t] = slot
    info_ref[t] = base
    count[0] = base + number
    first = base // BLOCK
    last = jnp.where(number > 0, (base + number - 1) // BLOCK + 1, first)
    zero = jnp.zeros_like(rcv)
    meta = jnp.concatenate([place, q & 31, rcv >> 7, rcv & 127, zero, zero, zero, zero], axis=0)
    meta = meta.astype(F32).astype(BF16)

    def gather(b, carry):
        hot = (iota((BLOCK, TILE), 0) + b * BLOCK == slot).astype(BF16)
        rows = pl.ds(pl.multiple_of(b * BLOCK, BLOCK), BLOCK)
        fresh = b * BLOCK >= base
        far_edges[rows] = jnp.where(fresh, 0.0, far_edges[rows]) + dot(hot, edges_ref[pl.ds(pl.multiple_of(t * TILE, TILE), TILE)]).astype(BF16)
        far_meta[b] = jnp.where(fresh, 0.0, far_meta[b]) + dot_last(meta, hot)
        return carry

    lax.fori_loop(first, last, gather, 0)


def near_kernel(begin, end, pieces, *refs):
    (
        snd_ref, rcv_ref, edges_ref, tr_ref,
        w_edge_ref, b1_ref, w2_ref, b2_ref, gain_ref, shift_ref,
    ) = refs[:10]
    window, snd_c, rcv_c, updates = refs[-4:]
    if begin == 0:
        spot_ref, own_ts_ref, h0_ref, h1_ref, h2_ref, h3_ref, w_sender_ref = refs[10:17]
        new_edges_ref, agg_ref, ts_ref = refs[17:20]
        w_sender = w_sender_ref[...]
        ts_ref[:NODE] = own_ts_ref[...]
        core = spot_ref[3]
        for k, h_ref in zip((0, 1, 2 + core, 3 - core), (h0_ref, h1_ref, h2_ref, h3_ref)):
            there = pl.ds(pl.multiple_of(NODE + k * HALO, HALO), HALO)
            ts_ref[there] = dot(h_ref[...], w_sender).astype(BF16)
        agg_ref[...] = jnp.zeros_like(agg_ref)
    else:
        ts_ref = refs[10]
        ready = refs[13:13 + pieces]
        new_edges_ref, agg_ref = refs[13 + pieces:15 + pieces]
        if pieces:
            table, sems = refs[15 + pieces:17 + pieces]
        copies = [
            pltpu.make_async_copy(piece, table.at[k * 1024:(k + 1) * 1024], sems.at[k])
            for k, piece in enumerate(ready)
        ]
        for copy in copies:
            copy.start()
    window[WINDOW:] = tr_ref[NODE - 16:]

    def edge_rows(at, col, hots, tables):
        edges = edges_ref[at]
        pre = dot(edges, w_edge_ref[...]) + b1_ref[...]
        for hot, part in zip(hots, tables):
            pre = pre + dot(hot, part)
        hidden = silu(pre).astype(BF16)
        update = layer_norm(dot(hidden, w2_ref[...]) + b2_ref[...], gain_ref[...], shift_ref[...])
        new_edges_ref[at] = jnp.where(col >= 0, edges.astype(F32) + update, 0.0).astype(BF16)
        return update.astype(BF16)

    def columns(*rows):
        both = jnp.concatenate(list(rows) * 4, axis=0)
        cols = jnp.transpose(both.astype(F32), (1, 0)).astype(jnp.int32)
        return cols[:, 0:1], cols[:, 1:2]

    def step(i, carry):
        snd = snd_ref[i]
        rcv = rcv_ref[i]
        far = snd >= NEAR
        live = rcv < NODE
        low = jnp.min(rcv)
        high = jnp.max(jnp.where(live, rcv, -1))
        start = pl.multiple_of(jnp.minimum(low // 16 * 16, NODE - WINDOW), 16)
        narrow = high - start < WINDOW
        snd_n = jnp.where(far, -1, snd)

        @pl.when(narrow)
        def _():
            window[:WINDOW] = tr_ref[pl.ds(start, WINDOW)]
            snd_v, rcv_v = columns(snd_n, jnp.where(live, rcv - start, WINDOW + 15))
            parts = []
            for k in range(0, TILE, SUB):
                col = snd_v[k:k + SUB]
                hot_s = (iota((SUB, NEAR), 1) == col).astype(BF16)
                hot_r = (iota((SUB, 256), 1) == rcv_v[k:k + SUB]).astype(BF16)
                at = pl.ds(pl.multiple_of(i * TILE + k, SUB), SUB)
                parts.append(edge_rows(at, col, [hot_s, hot_r], [ts_ref[...], window[...]]))
            hot_n = (iota((WINDOW, TILE), 0) == jnp.where(far, -1, rcv - start)).astype(BF16)
            agg_ref[pl.ds(start, WINDOW)] += dot(hot_n, jnp.concatenate(parts, axis=0))

        @pl.when(jnp.logical_not(narrow))
        def _():
            snd_v, rcv_v = columns(snd_n, jnp.minimum(rcv, NODE - 1))
            snd_c[...] = snd_v
            rcv_c[...] = rcv_v

            def some(j, c):
                at = pl.ds(pl.multiple_of(j * 128, 128), 128)
                col = snd_c[at]
                hot_s = (iota((128, NEAR), 1) == col).astype(BF16)
                hot_r = (iota((128, NODE), 1) == rcv_c[at]).astype(BF16)
                there = pl.ds(pl.multiple_of(i * TILE + j * 128, 128), 128)
                updates[at] = edge_rows(there, col, [hot_s, hot_r], [ts_ref[...], tr_ref[...]])
                return c

            lax.fori_loop(0, TILE // 128, some, 0)

            def sums(j, c):
                at = pl.ds(pl.multiple_of(j * 128, 128), 128)
                hot_n = (iota((128, TILE), 0) + j * 128 == jnp.where(far, -1, rcv)).astype(BF16)
                agg_ref[at] += dot(hot_n, updates[...])
                return c

            lax.fori_loop(0, NODE // 128, sums, 0)

        return carry

    lax.fori_loop(begin, end, step, 0)
    if begin and pieces:
        for copy in copies:
            copy.wait()


def far_kernel(info_ref, code_ref, *refs):
    late = refs[1:1 + LATE]
    (
        _, far_edges_ref, far_pre_ref, agg_ref, slot_ref, rcv_ref, nodes_ref,
        w_sender, w2, w_self, w_aggr, wn2,
        b2_ref, gain_ref, shift_ref, bn1_ref, bn2_ref, gain_n_ref, shift_n_ref,
        new_nodes_ref, new_edges_ref, table, near,
        rows_buf, edges_buf, pre_buf, new_far, agg, sems, near_sems, row_sems,
    ) = refs[1 + LATE:]
    copies = [
        pltpu.make_async_copy(piece, table.at[(8 - LATE + k) * 1024:(9 - LATE + k) * 1024], sems.at[k])
        for k, piece in enumerate(late)
    ]

    def block_copies(b):
        rows = pl.ds(pl.multiple_of(b * SLOTS, SLOTS), SLOTS)
        return (
            pltpu.make_async_copy(far_edges_ref.at[rows], edges_buf, row_sems.at[0]),
            pltpu.make_async_copy(far_pre_ref.at[rows], pre_buf, row_sems.at[1]),
        )

    total = info_ref[TILES]
    for copy in copies:
        copy.start()

    @pl.when(total > 0)
    def _():
        for copy in block_copies(0):
            copy.start()

    agg[...] = agg_ref[...]
    inner_self = dot(nodes_ref[...].astype(BF16), w_self[...]) + bn1_ref[...]
    for copy in copies:
        copy.wait()

    def block(b, carry):
        @pl.when(b > 0)
        def _():
            for copy in block_copies(b):
                copy.start()

        count = jnp.minimum(SLOTS, (total - b * SLOTS + 15) // 16 * 16)

        row = b * (SLOTS // BLOCK)

        def gather(i, c):
            at, col, there = row + (i >> 4), (i & 15) * 16, pl.multiple_of(i * 64, 64)
            for k in range(16):
                rows_buf[pl.ds(there + k * 4, 4)] = table[code_ref[at, 0, col + k]].astype(F32)
            return c

        lax.fori_loop(0, count // 16, gather, 0)
        for copy in block_copies(b):
            copy.wait()
        for k in range(SLOTS // BLOCK):
            here = slice(k * BLOCK, (k + 1) * BLOCK)
            first = b * SLOTS + k * BLOCK
            valid = iota((BLOCK, 1), 0) + first < total
            sent = jnp.concatenate(
                [rows_buf[pl.ds(k * BLOCK * 4 + c, BLOCK, stride=4)] for c in range(4)], axis=1
            ).astype(BF16)
            pre = pre_buf[here] + dot(sent, w_sender[...])
            hidden = silu(pre).astype(BF16)
            update = layer_norm(dot(hidden, w2[...]) + b2_ref[...], gain_ref[...], shift_ref[...])
            update = jnp.where(valid, update, 0.0)
            new = jnp.where(valid, edges_buf[here].astype(F32) + update, 0.0)
            new_far[pl.ds(pl.multiple_of(first, BLOCK), BLOCK)] = new.astype(BF16)
            hot = (iota((NODE, BLOCK), 0) == rcv_ref[b * (SLOTS // BLOCK) + k]).astype(BF16)
            agg[...] += dot(hot, update.astype(BF16))
        return carry

    blocks = (total + SLOTS - 1) // SLOTS
    lax.fori_loop(0, blocks, block, 0)
    new_far[pl.ds(pl.multiple_of(blocks * SLOTS, SLOTS), BLOCK)] = jnp.zeros((BLOCK, D), BF16)

    def store(t):
        rows = pl.ds(pl.multiple_of(t * TILE, TILE), TILE)
        return pltpu.make_async_copy(near.at[rows], new_edges_ref.at[rows], near_sems.at[t])

    def tile(t, carry):
        base = info_ref[t]
        end = info_ref[t + 1]
        first = base // BLOCK
        last = jnp.where(end > base, (end - 1) // BLOCK + 1, first)
        rows = pl.ds(pl.multiple_of(t * TILE, TILE), TILE)
        slots = jnp.concatenate([slot_ref[t]] * 8, axis=0).astype(F32)
        slots = jnp.transpose(slots, (1, 0)).astype(jnp.int32)[:, 0:1]

        start = base // 16 * 16
        fits = end - start <= BLOCK

        def scatter(start):
            hot = (iota((TILE, BLOCK), 1) + start == slots).astype(BF16)
            there = pl.ds(pl.multiple_of(start, 16), BLOCK)
            near[rows] = near[rows] + dot(hot, new_far[there]).astype(BF16)

        @pl.when(jnp.logical_and(end > base, fits))
        def _():
            scatter(start)

        @pl.when(jnp.logical_not(fits))
        def _():
            def some(b, c):
                scatter(b * BLOCK)
                return c

            lax.fori_loop(first, last, some, 0)

        store(t).start()
        return carry

    lax.fori_loop(0, TILES, tile, 0)
    inner = silu(inner_self + dot(agg[...].astype(BF16), w_aggr[...])).astype(BF16)
    out = layer_norm(dot(inner, wn2[...]) + bn2_ref[...], gain_n_ref[...], shift_n_ref[...])
    new_nodes_ref[...] = nodes_ref[...] + out
    for t in range(TILES):
        store(t).wait()


def full(shape):
    return pl.BlockSpec(shape, lambda *_: (0,) * len(shape))


ANY = pl.BlockSpec(memory_space=pl.ANY)
SMEM = pl.BlockSpec(memory_space=pltpu.SMEM)
VMEM = pl.BlockSpec(memory_space=pltpu.VMEM)
HBM = pl.BlockSpec(memory_space=pltpu.HBM)
ROW = pl.BlockSpec((1, 1, TILE), lambda t: (t, 0, 0))
EDGES = pl.BlockSpec((TILE, D), lambda t: (t, 0))
SQUARE = full((D, D))
VECTOR = full((1, D))


def kept(dims, kind):
    return pltpu.VMEM(dims, kind)


def keep(array):
    return pltpu.with_memory_space_constraint(array, pltpu.VMEM)


def far_away(array):
    return pltpu.with_memory_space_constraint(array, pltpu.HBM)


def shape(dims, kind):
    return jax.ShapeDtypeStruct(dims, kind)


def load_kernel(*refs):
    count = (len(refs) - 1) // 2
    copies = [pltpu.make_async_copy(refs[k], refs[count + k], refs[-1].at[k]) for k in range(count)]
    for copy in copies:
        copy.start()
    for copy in copies:
        copy.wait()


def load(*arrays):
    count = len(arrays)
    return pl.pallas_call(
        load_kernel,
        in_specs=[HBM] * count,
        out_specs=[VMEM] * count,
        out_shape=[kept(array.shape, array.dtype) for array in arrays],
        scratch_shapes=[pltpu.SemaphoreType.DMA((count,))],
        compiler_params=pltpu.CompilerParams(vmem_limit_bytes=16 << 20),
        cost_estimate=pl.CostEstimate(flops=0, bytes_accessed=16 << 20, transcendentals=0),
    )(*(far_away(array) for array in arrays))


def pick(spot, nodes, send_rows):
    return pl.pallas_call(
        pick_kernel,
        in_specs=[SMEM, HBM, HBM],
        out_specs=[VMEM] * 6,
        out_shape=(kept((NODE, D), F32), kept((NODE, D), BF16)) + (shape((HALO, D), BF16),) * 4,
        scratch_shapes=[pltpu.VMEM((4, HALO), jnp.int32), pltpu.SemaphoreType.DMA((2,))],
        compiler_params=pltpu.CompilerParams(vmem_limit_bytes=16 << 20),
        cost_estimate=pl.CostEstimate(flops=2 * NODE * D * 256, bytes_accessed=2 << 20, transcendentals=0),
    )(spot, far_away(nodes), far_away(send_rows))


def compact(*args):
    rows = BLOCKS * BLOCK
    return pl.pallas_call(
        compact_kernel,
        in_specs=[SMEM] + [VMEM] * (len(args) - 1),
        out_specs=[VMEM, SMEM, VMEM, VMEM, VMEM, VMEM, HBM, HBM],
        out_shape=(
            kept((TILES, 1, TILE), jnp.int32), shape((16,), jnp.int32),
            shape((BLOCKS, 1, BLOCK), jnp.int32), kept((BLOCKS, 1, BLOCK), jnp.int32),
            kept((NODE, D), BF16), kept((NODE, D), BF16),
            pltpu.HBM((rows, D), BF16), pltpu.HBM((rows, D), F32),
        ),
        scratch_shapes=[
            pltpu.VMEM((256, 256), BF16), pltpu.VMEM((rows, D), BF16),
            pltpu.VMEM((BLOCKS, 8, BLOCK), F32), pltpu.VMEM((rows, D), F32),
            pltpu.SMEM((1,), jnp.int32), pltpu.SemaphoreType.DMA((BLOCKS, 2)),
        ],
        compiler_params=pltpu.CompilerParams(vmem_limit_bytes=30 << 20),
        cost_estimate=pl.CostEstimate(flops=4 << 30, bytes_accessed=8 << 20, transcendentals=0),
    )(*args)


def near(begin, end, pieces, *args):
    outs = [kept((EDGE, D), BF16), kept((NODE, D), F32)]
    scratch = [
        pltpu.VMEM((256, D), BF16), pltpu.VMEM((TILE, 1), jnp.int32), pltpu.VMEM((TILE, 1), jnp.int32),
        pltpu.VMEM((TILE, D), BF16),
    ]
    if begin == 0:
        outs = outs + [kept((NEAR, D), BF16)]
    if pieces:
        outs = outs + [kept((8192, 4, 128), BF16)]
        scratch = [pltpu.SemaphoreType.DMA((pieces,))] + scratch
    return pl.pallas_call(
        functools.partial(near_kernel, begin, end, pieces),
        in_specs=[SMEM if k == 10 and begin == 0 else VMEM for k in range(len(args))],
        out_specs=[VMEM] * len(outs),
        out_shape=outs,
        scratch_shapes=scratch,
        input_output_aliases={11: 0, 12: 1} if begin else {},
        compiler_params=pltpu.CompilerParams(vmem_limit_bytes=16 << 20),
        cost_estimate=pl.CostEstimate(flops=(end - begin) << 31, bytes_accessed=(end - begin) << 21, transcendentals=0),
    )(*args)


def far(*args):
    return pl.pallas_call(
        far_kernel,
        in_specs=[SMEM] * 2 + [VMEM] + [ANY] * LATE + [VMEM] + [HBM] * 2 + [VMEM] * (len(args) - 6 - LATE),
        out_specs=[VMEM, ANY, VMEM, VMEM],
        out_shape=(shape((NODE, D), F32), shape((EDGE, D), BF16), kept((8192, 4, 128), BF16), kept((EDGE, D), BF16)),
        input_output_aliases={2: 2, 3 + LATE: 3},
        scratch_shapes=[
            pltpu.VMEM((4 * SLOTS, 128), F32),
            pltpu.VMEM((SLOTS, D), BF16), pltpu.VMEM((SLOTS, D), F32), pltpu.VMEM(((BLOCKS + 1) * BLOCK, D), BF16),
            pltpu.VMEM((NODE, D), F32),
            pltpu.SemaphoreType.DMA((LATE,)), pltpu.SemaphoreType.DMA((TILES,)), pltpu.SemaphoreType.DMA((2,)),
        ],
        compiler_params=pltpu.CompilerParams(vmem_limit_bytes=24 << 20),
        cost_estimate=pl.CostEstimate(flops=4 << 30, bytes_accessed=24 << 20, transcendentals=1 << 20),
    )(*args)


def body(
    nodes, edges, sender, receiver, send_rows,
    w_sender, w_receiver, w_edge, bias_edge1, w_edge2, bias_edge2, gain_edge, shift_edge,
    w_node_self, w_node_aggr, bias_node1, w_node2, bias_node2, gain_node, shift_node,
):
    row = lambda v: v.reshape(1, D)
    tiles = lambda v: v.reshape(TILES, 1, TILE)
    after = lambda v, *first: lax.optimization_barrier((v,) + first)[0]
    x, c, y, z = (lax.axis_index(a) for a in AXES)
    spot = jnp.stack([x, y, z, c]).astype(jnp.int32)
    held = nodes[:COARSE_DEV].astype(BF16).reshape(COARSE_DEV, 4, 128)
    nodes, own, *out = pick(spot, nodes, send_rows)
    nodes, own = keep(nodes), keep(own)
    tables = jnp.asarray(np.repeat(PLACES.reshape(2, 1, 256), 8, axis=1), BF16)
    place = jnp.where(c == 0, tables[0], tables[1])

    def grow(held, stage, *first):
        got = [from_chip(held, pair) for pair in stage]
        return jnp.concatenate([after(held, *first)] + got, axis=0)

    held = after(grow(held, STAGES[0]), own)
    halo = [shift_patch(after(out[0], held), 1), shift_patch(after(out[1], held), -1)]
    names = load(
        after(edges, held), tiles(sender), tiles(receiver), w_sender, w_edge, w_edge2, w_receiver,
        w_node_self, w_node_aggr, w_node2,
        row(bias_edge1), row(bias_edge2), row(gain_edge), row(shift_edge),
        row(bias_node1), row(bias_node2), row(gain_node), row(shift_node),
    )
    (
        edges, snd, rcv, w_sender, w_edge, w_edge2, w_receiver, w_node_self, w_node_aggr, w_node2,
        bias_edge1, *vectors,
    ) = (keep(v) for v in names)
    edge_vectors, node_vectors = vectors[:3], vectors[3:]

    def edge_part(begin, end, pieces, *extra):
        outs = near(begin, end, pieces, snd, rcv, edges, tr, w_edge, bias_edge1, w_edge2, *edge_vectors, *extra)
        return [keep(v) for v in outs]

    held = after(grow(held, STAGES[1]), edges, *halo)
    halo = halo + [next_chip(after(out[2], held)), other_core(after(out[3], held))]
    slot, info, far_code, far_rcv, own_ts, tr, far_edges, far_pre = compact(
        spot, snd, rcv, edges, keep(after(own, held)), w_sender, w_receiver, w_edge, bias_edge1, place,
    )
    slot, far_rcv, own_ts, tr = (keep(v) for v in (slot, far_rcv, own_ts, tr))
    held = grow(held, STAGES[2], tr, *halo)
    last = [from_chip(held, pair) for pair in LAST]
    done, agg, ts = edge_part(0, 2, 0, spot, keep(after(own_ts, held)), *halo, w_sender)
    first = [other_core(held), other_core(after(last[0], agg))]
    done, agg = edge_part(2, 3, 0, ts, done, agg)
    second = [other_core(after(piece, agg)) for piece in last[1:]]
    early = [held, *last, *first]
    done, agg, table = edge_part(3, 4, 6, ts, done, agg, *early)
    new_nodes, new_edges, _, _ = far(
        info, far_code, table, *second, done,
        far_away(far_edges), far_away(far_pre), agg, slot, far_rcv, nodes,
        w_sender, w_edge2, w_node_self, w_node_aggr, w_node2, *edge_vectors, *node_vectors,
    )
    return new_nodes, new_edges


def solution(mesh):
    grid = Mesh(mesh.devices.reshape(SIZES), AXES)
    split = P(AXES, None)
    return jax.shard_map(
        body,
        mesh=grid,
        in_specs=(split, split, P(AXES), P(AXES), split) + (P(),) * 15,
        out_specs=(split, split),
        check_vma=False,
    )
```

```python
import functools

import numpy as np
import jax
import jax.numpy as jnp
from jax import lax
from jax.experimental import pallas as pl
from jax.experimental.pallas import tpu as pltpu
from jax.sharding import Mesh, PartitionSpec as P

AXES = ("x", "core", "y", "z")
SIZES = (4, 2, 4, 8)
NODE = 512
HALO = 64
NEAR = NODE + 4 * HALO
COARSE_DEV = 32
D = 512
EDGE = 4096
TILE = 1024
TILES = EDGE // TILE
BLOCK = 256
SLOTS = 768
BLOCKS = 18
LATE = 2
WINDOW = 240
SUB = 512
F32 = jnp.float32
BF16 = jnp.bfloat16

STAGES = (
    (((0, 0, 4),) * 2,),
    (((2, 0, 0), (0, 2, 0)), ((0, 2, 0), (2, 0, 0)), ((2, 2, 0),) * 2),
    (((1, 1, 1), (-1, -1, -1)), ((-1, -1, -1), (1, 1, 1)), ((0, 0, 2), (0, 0, -2))),
)
LAST = (((1, 0, 0), (-1, 0, 0)), ((0, 1, 0), (0, -1, 0)), ((0, 0, 1), (0, 0, -1)))


def places():
    own = np.zeros((2, 128), np.int32)
    for core in range(2):
        held = [(0, 0, 0)]
        for stage in STAGES + (LAST,):
            held = [
                ((a[0] + o[0]) % 4, (a[1] + o[1]) % 4, (a[2] + o[2]) % 8)
                for o in [(0, 0, 0)] + [pair[core] for pair in stage]
                for a in held
            ]
        assert len(set(held)) == 128
        for block, (x, y, z) in enumerate(held):
            own[core, x * 32 + y * 8 + z] = block
    return np.stack([np.stack([own[c] if c == k else 128 + own[k] for k in range(2)]) for c in range(2)])


PLACES = places()


def device(x, c, y, z):
    return ((x % 4) * 2 + c % 2) * 32 + (y % 4) * 8 + z % 8


def receive(block, source):
    spots = [(x, c, y, z) for x in range(4) for c in range(2) for y in range(4) for z in range(8)]
    return lax.ppermute(block, AXES, [(device(*source(*spot)), device(*spot)) for spot in spots])


def from_chip(block, pair):
    return receive(block, lambda x, c, y, z: (x + pair[c][0], c, y + pair[c][1], z + pair[c][2]))


def other_core(block):
    return receive(block, lambda x, c, y, z: (x, 1 - c, y, z))


def shift_patch(block, step):
    def source(x, c, y, z):
        j = (y * 8 + z - step) % 32
        return x, c, j // 8, j % 8

    return receive(block, source)


def next_chip(block):
    return receive(block, lambda x, c, y, z: (x - 1 + 2 * c, 1 - c, y, z))


def dot(a, b):
    return jnp.dot(a, b, preferred_element_type=F32)


def dot_first(a, b):
    return lax.dot_general(a, b, (((0,), (0,)), ((), ())), preferred_element_type=F32)


def dot_last(a, b):
    return lax.dot_general(a, b, (((1,), (1,)), ((), ())), preferred_element_type=F32)


def silu(v):
    half = 0.5 * v
    return half + half * jnp.tanh(half)


def layer_norm(v, gain, shift):
    center = v - jnp.mean(v, axis=-1, keepdims=True)
    spread = jnp.mean(center * center, axis=-1, keepdims=True)
    return center * lax.rsqrt(spread + 1e-05) * gain + shift


def iota(shape, dim):
    return lax.broadcasted_iota(jnp.int32, shape, dim)


def pick_kernel(spot_ref, nodes_in, rows_in, nodes_ref, own_ref, *refs):
    out_refs = refs[:4]
    rows_ref, sems = refs[4:]
    copies = [
        pltpu.make_async_copy(nodes_in, nodes_ref, sems.at[0]), pltpu.make_async_copy(rows_in, rows_ref, sems.at[1]),
    ]
    for copy in copies:
        copy.start()
    for copy in copies:
        copy.wait()
    own = nodes_ref[...].astype(BF16)
    own_ref[...] = own
    core = spot_ref[3]
    for row, out_ref in zip((0, 1, 3 - core, 2 + core), out_refs):
        hot = (iota((NODE, HALO), 0) == rows_ref[pl.ds(row, 1), :]).astype(BF16)
        out_ref[...] = dot_first(hot, own).astype(BF16)


def compact_kernel(
    spot_ref, snd_ref, rcv_ref, edges_ref, own_ref, w_sender_ref, w_receiver_ref, w_edge_ref, b1_ref, place_ref,
    slot_ref, info_ref, code_out_ref, rcv_out_ref, ts_ref, tr_ref, far_edges_ref, far_pre_ref,
    upper, far_edges, far_meta, far_pre, count, sems,
):
    ts_ref[...] = dot(own_ref[...], w_sender_ref[...]).astype(BF16)
    tr_ref[...] = dot(own_ref[...], w_receiver_ref[...]).astype(BF16)
    upper[...] = (iota((256, 256), 0) < iota((256, 256), 1)).astype(BF16)
    rcv_out_ref[...] = jnp.full_like(rcv_out_ref, NODE)
    count[0] = 0

    def tile(t, carry):
        compact_tile(
            t, spot_ref, snd_ref, rcv_ref, edges_ref, slot_ref, info_ref, upper, far_edges, far_meta, count,
        )
        return carry

    lax.fori_loop(0, TILES, tile, 0)
    total = count[0]
    info_ref[TILES] = total
    blocks = (total + BLOCK - 1) // BLOCK

    def copies(b):
        rows = pl.ds(pl.multiple_of(b * BLOCK, BLOCK), BLOCK)
        return (
            pltpu.make_async_copy(far_edges.at[rows], far_edges_ref.at[rows], sems.at[b, 0]),
            pltpu.make_async_copy(far_pre.at[rows], far_pre_ref.at[rows], sems.at[b, 1]),
        )

    def push(b, carry):
        info = far_meta[b].astype(jnp.int32)
        spots = (iota((256, BLOCK), 0) == info[0:1]).astype(BF16)
        mine = place_ref[pl.ds(pl.multiple_of(spot_ref[3] * 16, 16), 16)]
        block = dot(mine, spots)[0:1].astype(jnp.int32)
        code_out_ref[b] = block * 32 + info[1:2]
        live = iota((1, BLOCK), 1) + b * BLOCK < total
        rcv_b = jnp.where(live, info[2:3] * 128 + info[3:4], NODE)
        rcv_out_ref[b] = rcv_b
        rows = pl.ds(pl.multiple_of(b * BLOCK, BLOCK), BLOCK)
        hot = (iota((NODE, BLOCK), 0) == jnp.minimum(rcv_b, NODE - 1)).astype(BF16)
        far_pre[rows] = dot(far_edges[rows], w_edge_ref[...]) + dot_first(hot, tr_ref[...]) + b1_ref[...]
        for copy in copies(b):
            copy.start()
        return carry

    lax.fori_loop(0, blocks, push, 0)

    def settle(b, carry):
        for copy in copies(b):
            copy.wait()
        return carry

    lax.fori_loop(0, blocks, settle, 0)


def compact_tile(t, spot_ref, snd_ref, rcv_ref, edges_ref, slot_ref, info_ref, upper, far_edges, far_meta, count):
    rcv = rcv_ref[t]
    snd = snd_ref[t]
    far = snd >= NEAR
    q = jnp.maximum(snd - NEAR, 0)
    p = q >> 5
    dx = ((p >> 6) - spot_ref[0]) & 3
    dy = ((p >> 3) - spot_ref[1]) & 3
    dz = (p - spot_ref[2]) & 7
    place = (((p >> 5) & 1) << 7) | (dx << 5) | (dy << 3) | dz
    far_f = far.astype(F32)
    base = count[0]
    wide = jnp.broadcast_to(far_f, (8, TILE)).astype(BF16)
    before, passed = [], jnp.zeros((1, 1), F32)
    for k in range(0, TILE, 256):
        before.append(dot(wide[:, k:k + 256], upper[...])[0:1] + passed)
        passed = passed + jnp.sum(far_f[:, k:k + 256], axis=1, keepdims=True)
    before = jnp.concatenate(before, axis=1).astype(jnp.int32)
    number = jnp.sum(far_f).astype(jnp.int32)
    slot = jnp.where(far, base + before, -1)
    slot_ref[t] = slot
    info_ref[t] = base
    count[0] = base + number
    first = base // BLOCK
    last = jnp.where(number > 0, (base + number - 1) // BLOCK + 1, first)
    zero = jnp.zeros_like(rcv)
    meta = jnp.concatenate([place, q & 31, rcv >> 7, rcv & 127, zero, zero, zero, zero], axis=0)
    meta = meta.astype(F32).astype(BF16)

    def gather(b, carry):
        hot = (iota((BLOCK, TILE), 0) + b * BLOCK == slot).astype(BF16)
        rows = pl.ds(pl.multiple_of(b * BLOCK, BLOCK), BLOCK)
        fresh = b * BLOCK >= base
        far_edges[rows] = jnp.where(fresh, 0.0, far_edges[rows]) + dot(hot, edges_ref[pl.ds(pl.multiple_of(t * TILE, TILE), TILE)]).astype(BF16)
        far_meta[b] = jnp.where(fresh, 0.0, far_meta[b]) + dot_last(meta, hot)
        return carry

    lax.fori_loop(first, last, gather, 0)


def near_kernel(begin, whole, half, pieces, *refs):
    (
        snd_ref, rcv_ref, edges_ref, tr_ref,
        w_edge_ref, b1_ref, w2_ref, b2_ref, gain_ref, shift_ref,
    ) = refs[:10]
    window, snd_c, rcv_c, updates = refs[-4:]
    if begin == 0:
        spot_ref, own_ts_ref, h0_ref, h1_ref, h2_ref, h3_ref, w_sender_ref = refs[10:17]
        new_edges_ref, agg_ref, ts_ref = refs[17:20]
        w_sender = w_sender_ref[...]
        ts_ref[:NODE] = own_ts_ref[...]
        core = spot_ref[3]
        for k, h_ref in zip((0, 1, 2 + core, 3 - core), (h0_ref, h1_ref, h2_ref, h3_ref)):
            there = pl.ds(pl.multiple_of(NODE + k * HALO, HALO), HALO)
            ts_ref[there] = dot(h_ref[...], w_sender).astype(BF16)
        agg_ref[...] = jnp.zeros_like(agg_ref)
    else:
        ts_ref = refs[10]
        ready = refs[13:13 + pieces]
        new_edges_ref, agg_ref = refs[13 + pieces:15 + pieces]
        if pieces:
            table, sems = refs[15 + pieces:17 + pieces]
        copies = [
            pltpu.make_async_copy(piece, table.at[k * 1024:(k + 1) * 1024], sems.at[k])
            for k, piece in enumerate(ready)
        ]
        for copy in copies:
            copy.start()
    window[WINDOW:] = tr_ref[NODE - 16:]

    def edge_rows(at, col, hots, tables):
        edges = edges_ref[at]
        pre = dot(edges, w_edge_ref[...]) + b1_ref[...]
        for hot, part in zip(hots, tables):
            pre = pre + dot(hot, part)
        hidden = silu(pre).astype(BF16)
        update = layer_norm(dot(hidden, w2_ref[...]) + b2_ref[...], gain_ref[...], shift_ref[...])
        new_edges_ref[at] = jnp.where(col >= 0, edges.astype(F32) + update, 0.0).astype(BF16)
        return update.astype(BF16)

    def columns(*rows):
        both = jnp.concatenate(list(rows) * 4, axis=0)
        cols = jnp.transpose(both.astype(F32), (1, 0)).astype(jnp.int32)
        return cols[:, 0:1], cols[:, 1:2]

    def step(unit, size):
        units = range(size // SUB)
        snd = jnp.concatenate([snd_ref[unit + k] for k in units], axis=1)
        rcv = jnp.concatenate([rcv_ref[unit + k] for k in units], axis=1)
        far = snd >= NEAR
        live = rcv < NODE
        low = jnp.min(rcv)
        high = jnp.max(jnp.where(live, rcv, -1))
        start = pl.multiple_of(jnp.minimum(low // 16 * 16, NODE - WINDOW), 16)
        narrow = high - start < WINDOW
        snd_n = jnp.where(far, -1, snd)

        @pl.when(narrow)
        def _():
            window[:WINDOW] = tr_ref[pl.ds(start, WINDOW)]
            snd_v, rcv_v = columns(snd_n, jnp.where(live, rcv - start, WINDOW + 15))
            parts = []
            for k in range(0, size, SUB):
                col = snd_v[k:k + SUB]
                hot_s = (iota((SUB, NEAR), 1) == col).astype(BF16)
                hot_r = (iota((SUB, 256), 1) == rcv_v[k:k + SUB]).astype(BF16)
                at = pl.ds(pl.multiple_of(unit * SUB + k, SUB), SUB)
                parts.append(edge_rows(at, col, [hot_s, hot_r], [ts_ref[...], window[...]]))
            hot_n = (iota((WINDOW, size), 0) == jnp.where(far, -1, rcv - start)).astype(BF16)
            agg_ref[pl.ds(start, WINDOW)] += dot(hot_n, jnp.concatenate(parts, axis=0))

        @pl.when(jnp.logical_not(narrow))
        def _():
            snd_v, rcv_v = columns(snd_n, jnp.minimum(rcv, NODE - 1))
            snd_c[:size] = snd_v
            rcv_c[:size] = rcv_v

            def some(j, c):
                at = pl.ds(pl.multiple_of(j * 128, 128), 128)
                col = snd_c[at]
                hot_s = (iota((128, NEAR), 1) == col).astype(BF16)
                hot_r = (iota((128, NODE), 1) == rcv_c[at]).astype(BF16)
                there = pl.ds(pl.multiple_of(unit * SUB + j * 128, 128), 128)
                updates[at] = edge_rows(there, col, [hot_s, hot_r], [ts_ref[...], tr_ref[...]])
                return c

            lax.fori_loop(0, size // 128, some, 0)

            def sums(j, c):
                at = pl.ds(pl.multiple_of(j * 128, 128), 128)
                hot_n = (iota((128, size), 0) + j * 128 == jnp.where(far, -1, rcv)).astype(BF16)
                agg_ref[at] += dot(hot_n, updates[:size])
                return c

            lax.fori_loop(0, NODE // 128, sums, 0)

    def tile(i, carry):
        step(begin + 2 * i, TILE)
        return carry

    if whole:
        lax.fori_loop(0, whole, tile, 0)
    if half:
        step(begin + 2 * whole, SUB)
    if begin and pieces:
        for copy in copies:
            copy.wait()


def far_kernel(info_ref, code_ref, *refs):
    late = refs[1:1 + LATE]
    (
        _, far_edges_ref, far_pre_ref, agg_ref, slot_ref, rcv_ref, nodes_ref,
        w_sender, w2, w_self, w_aggr, wn2,
        b2_ref, gain_ref, shift_ref, bn1_ref, bn2_ref, gain_n_ref, shift_n_ref,
        new_nodes_ref, new_edges_ref, table, near,
        rows_buf, edges_buf, pre_buf, new_far, agg, sems, near_sems, row_sems,
    ) = refs[1 + LATE:]
    copies = [
        pltpu.make_async_copy(piece, table.at[(8 - LATE + k) * 1024:(9 - LATE + k) * 1024], sems.at[k])
        for k, piece in enumerate(late)
    ]

    def block_copies(b):
        rows = pl.ds(pl.multiple_of(b * SLOTS, SLOTS), SLOTS)
        return (
            pltpu.make_async_copy(far_edges_ref.at[rows], edges_buf, row_sems.at[0]),
            pltpu.make_async_copy(far_pre_ref.at[rows], pre_buf, row_sems.at[1]),
        )

    total = info_ref[TILES]
    for copy in copies:
        copy.start()

    @pl.when(total > 0)
    def _():
        for copy in block_copies(0):
            copy.start()

    agg[...] = agg_ref[...]
    inner_self = dot(nodes_ref[...].astype(BF16), w_self[...]) + bn1_ref[...]
    for copy in copies:
        copy.wait()

    def block(b, carry):
        @pl.when(b > 0)
        def _():
            for copy in block_copies(b):
                copy.start()

        count = jnp.minimum(SLOTS, (total - b * SLOTS + 15) // 16 * 16)

        row = b * (SLOTS // BLOCK)

        def gather(i, c):
            at, col, there = row + (i >> 4), (i & 15) * 16, pl.multiple_of(i * 64, 64)
            for k in range(16):
                rows_buf[pl.ds(there + k * 4, 4)] = table[code_ref[at, 0, col + k]].astype(F32)
            return c

        lax.fori_loop(0, count // 16, gather, 0)
        for copy in block_copies(b):
            copy.wait()
        for k in range(SLOTS // BLOCK):
            here = slice(k * BLOCK, (k + 1) * BLOCK)
            first = b * SLOTS + k * BLOCK
            valid = iota((BLOCK, 1), 0) + first < total
            sent = jnp.concatenate(
                [rows_buf[pl.ds(k * BLOCK * 4 + c, BLOCK, stride=4)] for c in range(4)], axis=1
            ).astype(BF16)
            pre = pre_buf[here] + dot(sent, w_sender[...])
            hidden = silu(pre).astype(BF16)
            update = layer_norm(dot(hidden, w2[...]) + b2_ref[...], gain_ref[...], shift_ref[...])
            update = jnp.where(valid, update, 0.0)
            new = jnp.where(valid, edges_buf[here].astype(F32) + update, 0.0)
            new_far[pl.ds(pl.multiple_of(first, BLOCK), BLOCK)] = new.astype(BF16)
            hot = (iota((NODE, BLOCK), 0) == rcv_ref[b * (SLOTS // BLOCK) + k]).astype(BF16)
            agg[...] += dot(hot, update.astype(BF16))
        return carry

    blocks = (total + SLOTS - 1) // SLOTS
    lax.fori_loop(0, blocks, block, 0)
    new_far[pl.ds(pl.multiple_of(blocks * SLOTS, SLOTS), BLOCK)] = jnp.zeros((BLOCK, D), BF16)

    def store(t):
        rows = pl.ds(pl.multiple_of(t * TILE, TILE), TILE)
        return pltpu.make_async_copy(near.at[rows], new_edges_ref.at[rows], near_sems.at[t])

    def tile(t, carry):
        base = info_ref[t]
        end = info_ref[t + 1]
        first = base // BLOCK
        last = jnp.where(end > base, (end - 1) // BLOCK + 1, first)
        rows = pl.ds(pl.multiple_of(t * TILE, TILE), TILE)
        slots = jnp.concatenate([slot_ref[t]] * 8, axis=0).astype(F32)
        slots = jnp.transpose(slots, (1, 0)).astype(jnp.int32)[:, 0:1]

        start = base // 16 * 16
        fits = end - start <= BLOCK

        def scatter(start):
            hot = (iota((TILE, BLOCK), 1) + start == slots).astype(BF16)
            there = pl.ds(pl.multiple_of(start, 16), BLOCK)
            near[rows] = near[rows] + dot(hot, new_far[there]).astype(BF16)

        @pl.when(jnp.logical_and(end > base, fits))
        def _():
            scatter(start)

        @pl.when(jnp.logical_not(fits))
        def _():
            def some(b, c):
                scatter(b * BLOCK)
                return c

            lax.fori_loop(first, last, some, 0)

        store(t).start()
        return carry

    lax.fori_loop(0, TILES, tile, 0)
    inner = silu(inner_self + dot(agg[...].astype(BF16), w_aggr[...])).astype(BF16)
    out = layer_norm(dot(inner, wn2[...]) + bn2_ref[...], gain_n_ref[...], shift_n_ref[...])
    new_nodes_ref[...] = nodes_ref[...] + out
    for t in range(TILES):
        store(t).wait()


def full(shape):
    return pl.BlockSpec(shape, lambda *_: (0,) * len(shape))


ANY = pl.BlockSpec(memory_space=pl.ANY)
SMEM = pl.BlockSpec(memory_space=pltpu.SMEM)
VMEM = pl.BlockSpec(memory_space=pltpu.VMEM)
HBM = pl.BlockSpec(memory_space=pltpu.HBM)
ROW = pl.BlockSpec((1, 1, TILE), lambda t: (t, 0, 0))
EDGES = pl.BlockSpec((TILE, D), lambda t: (t, 0))
SQUARE = full((D, D))
VECTOR = full((1, D))


def kept(dims, kind):
    return pltpu.VMEM(dims, kind)


def keep(array):
    return pltpu.with_memory_space_constraint(array, pltpu.VMEM)


def far_away(array):
    return pltpu.with_memory_space_constraint(array, pltpu.HBM)


def shape(dims, kind):
    return jax.ShapeDtypeStruct(dims, kind)


def load_kernel(*refs):
    count = (len(refs) - 1) // 2
    copies = [pltpu.make_async_copy(refs[k], refs[count + k], refs[-1].at[k]) for k in range(count)]
    for copy in copies:
        copy.start()
    for copy in copies:
        copy.wait()


def load(*arrays):
    count = len(arrays)
    return pl.pallas_call(
        load_kernel,
        in_specs=[HBM] * count,
        out_specs=[VMEM] * count,
        out_shape=[kept(array.shape, array.dtype) for array in arrays],
        scratch_shapes=[pltpu.SemaphoreType.DMA((count,))],
        compiler_params=pltpu.CompilerParams(vmem_limit_bytes=16 << 20),
        cost_estimate=pl.CostEstimate(flops=0, bytes_accessed=16 << 20, transcendentals=0),
    )(*(far_away(array) for array in arrays))


def pick(spot, nodes, send_rows):
    return pl.pallas_call(
        pick_kernel,
        in_specs=[SMEM, HBM, HBM],
        out_specs=[VMEM] * 6,
        out_shape=(kept((NODE, D), F32), kept((NODE, D), BF16)) + (shape((HALO, D), BF16),) * 4,
        scratch_shapes=[pltpu.VMEM((4, HALO), jnp.int32), pltpu.SemaphoreType.DMA((2,))],
        compiler_params=pltpu.CompilerParams(vmem_limit_bytes=16 << 20),
        cost_estimate=pl.CostEstimate(flops=2 * NODE * D * 256, bytes_accessed=2 << 20, transcendentals=0),
    )(spot, far_away(nodes), far_away(send_rows))


def compact(*args):
    rows = BLOCKS * BLOCK
    return pl.pallas_call(
        compact_kernel,
        in_specs=[SMEM] + [VMEM] * (len(args) - 1),
        out_specs=[VMEM, SMEM, VMEM, VMEM, VMEM, VMEM, HBM, HBM],
        out_shape=(
            kept((TILES, 1, TILE), jnp.int32), shape((16,), jnp.int32),
            shape((BLOCKS, 1, BLOCK), jnp.int32), kept((BLOCKS, 1, BLOCK), jnp.int32),
            kept((NODE, D), BF16), kept((NODE, D), BF16),
            pltpu.HBM((rows, D), BF16), pltpu.HBM((rows, D), F32),
        ),
        scratch_shapes=[
            pltpu.VMEM((256, 256), BF16), pltpu.VMEM((rows, D), BF16),
            pltpu.VMEM((BLOCKS, 8, BLOCK), F32), pltpu.VMEM((rows, D), F32),
            pltpu.SMEM((1,), jnp.int32), pltpu.SemaphoreType.DMA((BLOCKS, 2)),
        ],
        compiler_params=pltpu.CompilerParams(vmem_limit_bytes=30 << 20),
        cost_estimate=pl.CostEstimate(flops=4 << 30, bytes_accessed=8 << 20, transcendentals=0),
    )(*args)


def near(begin, whole, half, pieces, *args):
    outs = [kept((EDGE, D), BF16), kept((NODE, D), F32)]
    scratch = [
        pltpu.VMEM((256, D), BF16), pltpu.VMEM((TILE, 1), jnp.int32), pltpu.VMEM((TILE, 1), jnp.int32),
        pltpu.VMEM((TILE, D), BF16),
    ]
    if begin == 0:
        outs = outs + [kept((NEAR, D), BF16)]
    if pieces:
        outs = outs + [kept((8192, 4, 128), BF16)]
        scratch = [pltpu.SemaphoreType.DMA((pieces,))] + scratch
    return pl.pallas_call(
        functools.partial(near_kernel, begin, whole, half, pieces),
        in_specs=[SMEM if k == 10 and begin == 0 else VMEM for k in range(len(args))],
        out_specs=[VMEM] * len(outs),
        out_shape=outs,
        scratch_shapes=scratch,
        input_output_aliases={11: 0, 12: 1} if begin else {},
        compiler_params=pltpu.CompilerParams(vmem_limit_bytes=16 << 20),
        cost_estimate=pl.CostEstimate(flops=(2 * whole + half) << 30, bytes_accessed=(2 * whole + half) << 20, transcendentals=0),
    )(*args)


def far(*args):
    return pl.pallas_call(
        far_kernel,
        in_specs=[SMEM] * 2 + [VMEM] + [ANY] * LATE + [VMEM] + [HBM] * 2 + [VMEM] * (len(args) - 6 - LATE),
        out_specs=[VMEM, ANY, VMEM, VMEM],
        out_shape=(shape((NODE, D), F32), shape((EDGE, D), BF16), kept((8192, 4, 128), BF16), kept((EDGE, D), BF16)),
        input_output_aliases={2: 2, 3 + LATE: 3},
        scratch_shapes=[
            pltpu.VMEM((4 * SLOTS, 128), F32),
            pltpu.VMEM((SLOTS, D), BF16), pltpu.VMEM((SLOTS, D), F32), pltpu.VMEM(((BLOCKS + 1) * BLOCK, D), BF16),
            pltpu.VMEM((NODE, D), F32),
            pltpu.SemaphoreType.DMA((LATE,)), pltpu.SemaphoreType.DMA((TILES,)), pltpu.SemaphoreType.DMA((2,)),
        ],
        compiler_params=pltpu.CompilerParams(vmem_limit_bytes=24 << 20),
        cost_estimate=pl.CostEstimate(flops=4 << 30, bytes_accessed=24 << 20, transcendentals=1 << 20),
    )(*args)


def body(
    nodes, edges, sender, receiver, send_rows,
    w_sender, w_receiver, w_edge, bias_edge1, w_edge2, bias_edge2, gain_edge, shift_edge,
    w_node_self, w_node_aggr, bias_node1, w_node2, bias_node2, gain_node, shift_node,
):
    row = lambda v: v.reshape(1, D)
    tiles = lambda v, size: v.reshape(EDGE // size, 1, size)
    after = lambda v, *first: lax.optimization_barrier((v,) + first)[0]
    x, c, y, z = (lax.axis_index(a) for a in AXES)
    spot = jnp.stack([x, y, z, c]).astype(jnp.int32)
    held = nodes[:COARSE_DEV].astype(BF16).reshape(COARSE_DEV, 4, 128)
    nodes, own, *out = pick(spot, nodes, send_rows)
    nodes, own = keep(nodes), keep(own)
    place = jnp.asarray(np.repeat(PLACES.reshape(2, 256), 16, axis=0), BF16)

    def grow(held, stage, *first):
        got = [from_chip(held, pair) for pair in stage]
        return jnp.concatenate([after(held, *first)] + got, axis=0)

    held = after(grow(held, STAGES[0]), own)
    halo = [shift_patch(after(out[0], held), 1), shift_patch(after(out[1], held), -1)]
    names = load(
        after(edges, held), tiles(sender, SUB), tiles(receiver, SUB), tiles(sender, TILE), tiles(receiver, TILE), w_sender, w_edge, w_edge2, w_receiver,
        w_node_self, w_node_aggr, w_node2,
        row(bias_edge1), row(bias_edge2), row(gain_edge), row(shift_edge),
        row(bias_node1), row(bias_node2), row(gain_node), row(shift_node), place,
    )
    (
        edges, snd, rcv, snd_t, rcv_t, w_sender, w_edge, w_edge2, w_receiver, w_node_self, w_node_aggr, w_node2,
        bias_edge1, *vectors, place,
    ) = (keep(v) for v in names)
    edge_vectors, node_vectors = vectors[:3], vectors[3:]

    def edge_part(begin, whole, half, pieces, *extra):
        outs = near(begin, whole, half, pieces, snd, rcv, edges, tr, w_edge, bias_edge1, w_edge2, *edge_vectors, *extra)
        return [keep(v) for v in outs]

    held = after(grow(held, STAGES[1]), edges, *halo)
    halo = halo + [next_chip(after(out[2], held)), other_core(after(out[3], held))]
    slot, info, far_code, far_rcv, own_ts, tr, far_edges, far_pre = compact(
        spot, snd_t, rcv_t, edges, keep(after(own, held)), w_sender, w_receiver, w_edge, bias_edge1, place,
    )
    slot, far_rcv, own_ts, tr = (keep(v) for v in (slot, far_rcv, own_ts, tr))
    held = grow(held, STAGES[2], tr, *halo)
    last = [from_chip(held, pair) for pair in LAST]
    done, agg, ts = edge_part(0, 2, 1, 0, spot, keep(after(own_ts, held)), *halo, w_sender)
    first = [other_core(held), other_core(after(last[0], agg))]
    done, agg = edge_part(5, 0, 1, 0, ts, done, agg)
    second = [other_core(after(piece, agg)) for piece in last[1:]]
    early = [held, *last, *first]
    done, agg, table = edge_part(6, 1, 0, 6, ts, done, agg, *early)
    new_nodes, new_edges, _, _ = far(
        info, far_code, table, *second, done,
        far_away(far_edges), far_away(far_pre), agg, slot, far_rcv, nodes,
        w_sender, w_edge2, w_node_self, w_node_aggr, w_node2, *edge_vectors, *node_vectors,
    )
    return new_nodes, new_edges


def solution(mesh):
    grid = Mesh(mesh.devices.reshape(SIZES), AXES)
    split = P(AXES, None)
    return jax.shard_map(
        body,
        mesh=grid,
        in_specs=(split, split, P(AXES), P(AXES), split) + (P(),) * 15,
        out_specs=(split, split),
        check_vma=False,
    )
```

```python
import functools

import numpy as np
import jax
import jax.numpy as jnp
from jax import lax
from jax.experimental import pallas as pl
from jax.experimental.pallas import tpu as pltpu
from jax.sharding import Mesh, PartitionSpec as P

AXES = ("x", "core", "y", "z")
SIZES = (4, 2, 4, 8)
NODE = 512
HALO = 64
NEAR = NODE + 4 * HALO
COARSE_DEV = 32
D = 512
EDGE = 4096
TILE = 1024
TILES = EDGE // TILE
BLOCK = 256
SLOTS = 768
BLOCKS = 18
LATE = 2
WINDOW = 240
SUB = 512
F32 = jnp.float32
BF16 = jnp.bfloat16

STAGES = (
    (((0, 0, 4),) * 2,),
    (((2, 0, 0), (0, 2, 0)), ((0, 2, 0), (2, 0, 0)), ((2, 2, 0),) * 2),
    (((1, 1, 1), (-1, -1, -1)), ((-1, -1, -1), (1, 1, 1)), ((0, 0, 2), (0, 0, -2))),
)
LAST = (((1, 0, 0), (-1, 0, 0)), ((0, 1, 0), (0, -1, 0)), ((0, 0, 1), (0, 0, -1)))


def places():
    own = np.zeros((2, 128), np.int32)
    for core in range(2):
        held = [(0, 0, 0)]
        for stage in STAGES + (LAST,):
            held = [
                ((a[0] + o[0]) % 4, (a[1] + o[1]) % 4, (a[2] + o[2]) % 8)
                for o in [(0, 0, 0)] + [pair[core] for pair in stage]
                for a in held
            ]
        assert len(set(held)) == 128
        for block, (x, y, z) in enumerate(held):
            own[core, x * 32 + y * 8 + z] = block
    return np.stack([np.stack([own[c] if c == k else 128 + own[k] for k in range(2)]) for c in range(2)])


PLACES = places()


def device(x, c, y, z):
    return ((x % 4) * 2 + c % 2) * 32 + (y % 4) * 8 + z % 8


def receive(block, source):
    spots = [(x, c, y, z) for x in range(4) for c in range(2) for y in range(4) for z in range(8)]
    return lax.ppermute(block, AXES, [(device(*source(*spot)), device(*spot)) for spot in spots])


def from_chip(block, pair):
    return receive(block, lambda x, c, y, z: (x + pair[c][0], c, y + pair[c][1], z + pair[c][2]))


def other_core(block):
    return receive(block, lambda x, c, y, z: (x, 1 - c, y, z))


def shift_patch(block, step):
    def source(x, c, y, z):
        j = (y * 8 + z - step) % 32
        return x, c, j // 8, j % 8

    return receive(block, source)


def next_chip(block):
    return receive(block, lambda x, c, y, z: (x - 1 + 2 * c, 1 - c, y, z))


def dot(a, b):
    return jnp.dot(a, b, preferred_element_type=F32)


def dot_first(a, b):
    return lax.dot_general(a, b, (((0,), (0,)), ((), ())), preferred_element_type=F32)


def dot_last(a, b):
    return lax.dot_general(a, b, (((1,), (1,)), ((), ())), preferred_element_type=F32)


def silu(v):
    half = 0.5 * v
    return half + half * jnp.tanh(half)


def layer_norm(v, gain, shift):
    center = v - jnp.mean(v, axis=-1, keepdims=True)
    spread = jnp.mean(center * center, axis=-1, keepdims=True)
    return center * lax.rsqrt(spread + 1e-05) * gain + shift


def iota(shape, dim):
    return lax.broadcasted_iota(jnp.int32, shape, dim)


def pick_kernel(spot_ref, nodes_in, rows_in, nodes_ref, own_ref, *refs):
    out_refs = refs[:4]
    rows_ref, sems = refs[4:]
    copies = [
        pltpu.make_async_copy(nodes_in, nodes_ref, sems.at[0]), pltpu.make_async_copy(rows_in, rows_ref, sems.at[1]),
    ]
    for copy in copies:
        copy.start()
    for copy in copies:
        copy.wait()
    own = nodes_ref[...].astype(BF16)
    own_ref[...] = own
    core = spot_ref[3]
    for row, out_ref in zip((0, 1, 3 - core, 2 + core), out_refs):
        hot = (iota((NODE, HALO), 0) == rows_ref[pl.ds(row, 1), :]).astype(BF16)
        out_ref[...] = dot_first(hot, own).astype(BF16)


def compact_kernel(
    spot_ref, snd_ref, rcv_ref, edges_ref, own_ref, w_sender_ref, w_receiver_ref, w_edge_ref, b1_ref, place_ref,
    slot_ref, info_ref, code_out_ref, rcv_out_ref, ts_ref, tr_ref, far_edges_ref, far_pre_ref,
    upper, far_edges, far_meta, far_pre, count, sems,
):
    ts_ref[...] = dot(own_ref[...], w_sender_ref[...]).astype(BF16)
    tr_ref[...] = dot(own_ref[...], w_receiver_ref[...]).astype(BF16)
    upper[...] = (iota((256, 256), 0) < iota((256, 256), 1)).astype(BF16)
    rcv_out_ref[...] = jnp.full_like(rcv_out_ref, NODE)
    count[0] = 0

    def tile(t, carry):
        compact_tile(
            t, spot_ref, snd_ref, rcv_ref, edges_ref, slot_ref, info_ref, upper, far_edges, far_meta, count,
        )
        return carry

    lax.fori_loop(0, TILES, tile, 0)
    total = count[0]
    info_ref[TILES] = total
    blocks = (total + BLOCK - 1) // BLOCK

    def copies(b):
        rows = pl.ds(pl.multiple_of(b * BLOCK, BLOCK), BLOCK)
        return (
            pltpu.make_async_copy(far_edges.at[rows], far_edges_ref.at[rows], sems.at[b, 0]),
            pltpu.make_async_copy(far_pre.at[rows], far_pre_ref.at[rows], sems.at[b, 1]),
        )

    def push(b, carry):
        info = far_meta[b].astype(jnp.int32)
        spots = (iota((256, BLOCK), 0) == info[0:1]).astype(BF16)
        mine = place_ref[pl.ds(pl.multiple_of(spot_ref[3] * 16, 16), 16)]
        block = dot(mine, spots)[0:1].astype(jnp.int32)
        code_out_ref[b] = block * 32 + info[1:2]
        live = iota((1, BLOCK), 1) + b * BLOCK < total
        rcv_b = jnp.where(live, info[2:3] * 128 + info[3:4], NODE)
        rcv_out_ref[b] = rcv_b
        rows = pl.ds(pl.multiple_of(b * BLOCK, BLOCK), BLOCK)
        hot = (iota((NODE, BLOCK), 0) == jnp.minimum(rcv_b, NODE - 1)).astype(BF16)
        far_pre[rows] = dot(far_edges[rows], w_edge_ref[...]) + dot_first(hot, tr_ref[...]) + b1_ref[...]
        for copy in copies(b):
            copy.start()
        return carry

    lax.fori_loop(0, blocks, push, 0)

    def settle(b, carry):
        for copy in copies(b):
            copy.wait()
        return carry

    lax.fori_loop(0, blocks, settle, 0)


def compact_tile(t, spot_ref, snd_ref, rcv_ref, edges_ref, slot_ref, info_ref, upper, far_edges, far_meta, count):
    rcv = rcv_ref[t]
    snd = snd_ref[t]
    far = snd >= NEAR
    q = jnp.maximum(snd - NEAR, 0)
    p = q >> 5
    dx = ((p >> 6) - spot_ref[0]) & 3
    dy = ((p >> 3) - spot_ref[1]) & 3
    dz = (p - spot_ref[2]) & 7
    place = (((p >> 5) & 1) << 7) | (dx << 5) | (dy << 3) | dz
    far_f = far.astype(F32)
    base = count[0]
    wide = jnp.broadcast_to(far_f, (8, TILE)).astype(BF16)
    before, passed = [], jnp.zeros((1, 1), F32)
    for k in range(0, TILE, 256):
        before.append(dot(wide[:, k:k + 256], upper[...])[0:1] + passed)
        passed = passed + jnp.sum(far_f[:, k:k + 256], axis=1, keepdims=True)
    before = jnp.concatenate(before, axis=1).astype(jnp.int32)
    number = jnp.sum(far_f).astype(jnp.int32)
    slot = jnp.where(far, base + before, -1)
    slot_ref[t] = slot
    info_ref[t] = base
    count[0] = base + number
    first = base // BLOCK
    last = jnp.where(number > 0, (base + number - 1) // BLOCK + 1, first)
    zero = jnp.zeros_like(rcv)
    meta = jnp.concatenate([place, q & 31, rcv >> 7, rcv & 127, zero, zero, zero, zero], axis=0)
    meta = meta.astype(F32).astype(BF16)

    def gather(b, carry):
        hot = (iota((BLOCK, TILE), 0) + b * BLOCK == slot).astype(BF16)
        rows = pl.ds(pl.multiple_of(b * BLOCK, BLOCK), BLOCK)
        fresh = b * BLOCK >= base
        far_edges[rows] = jnp.where(fresh, 0.0, far_edges[rows]) + dot(hot, edges_ref[pl.ds(pl.multiple_of(t * TILE, TILE), TILE)]).astype(BF16)
        far_meta[b] = jnp.where(fresh, 0.0, far_meta[b]) + dot_last(meta, hot)
        return carry

    lax.fori_loop(first, last, gather, 0)


def near_kernel(begin, whole, half, pieces, *refs):
    (
        snd_ref, rcv_ref, edges_ref, tr_ref,
        w_edge_ref, b1_ref, w2_ref, b2_ref, gain_ref, shift_ref,
    ) = refs[:10]
    window, snd_c, rcv_c, updates = refs[-4:]
    if begin == 0:
        spot_ref, own_ts_ref, h0_ref, h1_ref, h2_ref, h3_ref, w_sender_ref = refs[10:17]
        new_edges_ref, agg_ref, ts_ref = refs[17:20]
        w_sender = w_sender_ref[...]
        ts_ref[:NODE] = own_ts_ref[...]
        core = spot_ref[3]
        for k, h_ref in zip((0, 1, 2 + core, 3 - core), (h0_ref, h1_ref, h2_ref, h3_ref)):
            there = pl.ds(pl.multiple_of(NODE + k * HALO, HALO), HALO)
            ts_ref[there] = dot(h_ref[...], w_sender).astype(BF16)
        agg_ref[...] = jnp.zeros_like(agg_ref)
    else:
        ts_ref = refs[10]
        ready = refs[13:13 + pieces]
        new_edges_ref, agg_ref = refs[13 + pieces:15 + pieces]
        if pieces:
            table, sems = refs[15 + pieces:17 + pieces]
        copies = [
            pltpu.make_async_copy(piece, table.at[k * 1024:(k + 1) * 1024], sems.at[k])
            for k, piece in enumerate(ready)
        ]
        for copy in copies:
            copy.start()
    window[WINDOW:] = tr_ref[NODE - 16:]

    def edge_rows(at, col, hots, tables):
        edges = edges_ref[at]
        pre = dot(edges, w_edge_ref[...]) + b1_ref[...]
        for hot, part in zip(hots, tables):
            pre = pre + dot(hot, part)
        hidden = silu(pre).astype(BF16)
        update = layer_norm(dot(hidden, w2_ref[...]) + b2_ref[...], gain_ref[...], shift_ref[...])
        new_edges_ref[at] = jnp.where(col >= 0, edges.astype(F32) + update, 0.0).astype(BF16)
        return update.astype(BF16)

    def columns(*rows):
        both = jnp.concatenate(list(rows) * 4, axis=0)
        cols = jnp.transpose(both.astype(F32), (1, 0)).astype(jnp.int32)
        return cols[:, 0:1], cols[:, 1:2]

    def step(unit, size):
        units = range(size // SUB)
        snd = jnp.concatenate([snd_ref[unit + k] for k in units], axis=1)
        rcv = jnp.concatenate([rcv_ref[unit + k] for k in units], axis=1)
        far = snd >= NEAR
        live = rcv < NODE
        low = jnp.min(rcv)
        high = jnp.max(jnp.where(live, rcv, -1))
        start = pl.multiple_of(jnp.minimum(low // 16 * 16, NODE - WINDOW), 16)
        narrow = high - start < WINDOW
        snd_n = jnp.where(far, -1, snd)

        @pl.when(narrow)
        def _():
            window[:WINDOW] = tr_ref[pl.ds(start, WINDOW)]
            snd_v, rcv_v = columns(snd_n, jnp.where(live, rcv - start, WINDOW + 15))
            parts = []
            for k in range(0, size, SUB):
                col = snd_v[k:k + SUB]
                hot_s = (iota((SUB, NEAR), 1) == col).astype(BF16)
                hot_r = (iota((SUB, 256), 1) == rcv_v[k:k + SUB]).astype(BF16)
                at = pl.ds(pl.multiple_of(unit * SUB + k, SUB), SUB)
                parts.append(edge_rows(at, col, [hot_s, hot_r], [ts_ref[...], window[...]]))
            hot_n = (iota((WINDOW, size), 0) == jnp.where(far, -1, rcv - start)).astype(BF16)
            agg_ref[pl.ds(start, WINDOW)] += dot(hot_n, jnp.concatenate(parts, axis=0))

        @pl.when(jnp.logical_not(narrow))
        def _():
            snd_v, rcv_v = columns(snd_n, jnp.minimum(rcv, NODE - 1))
            snd_c[:size] = snd_v
            rcv_c[:size] = rcv_v

            def some(j, c):
                at = pl.ds(pl.multiple_of(j * 128, 128), 128)
                col = snd_c[at]
                hot_s = (iota((128, NEAR), 1) == col).astype(BF16)
                hot_r = (iota((128, NODE), 1) == rcv_c[at]).astype(BF16)
                there = pl.ds(pl.multiple_of(unit * SUB + j * 128, 128), 128)
                updates[at] = edge_rows(there, col, [hot_s, hot_r], [ts_ref[...], tr_ref[...]])
                return c

            lax.fori_loop(0, size // 128, some, 0)

            def sums(j, c):
                at = pl.ds(pl.multiple_of(j * 128, 128), 128)
                hot_n = (iota((128, size), 0) + j * 128 == jnp.where(far, -1, rcv)).astype(BF16)
                agg_ref[at] += dot(hot_n, updates[:size])
                return c

            lax.fori_loop(0, NODE // 128, sums, 0)

    def tile(i, carry):
        step(begin + 2 * i, TILE)
        return carry

    if whole:
        lax.fori_loop(0, whole, tile, 0)
    if half:
        step(begin + 2 * whole, SUB)
    if begin and pieces:
        for copy in copies:
            copy.wait()


def far_kernel(info_ref, code_ref, *refs):
    late = refs[1:1 + LATE]
    (
        _, far_edges_ref, far_pre_ref, agg_ref, slot_ref, rcv_ref, nodes_ref,
        w_sender, w2, w_self, w_aggr, wn2,
        b2_ref, gain_ref, shift_ref, bn1_ref, bn2_ref, gain_n_ref, shift_n_ref,
        new_nodes_ref, new_edges_ref, table, near,
        rows_buf, edges_buf, pre_buf, new_far, agg, sems, near_sems, row_sems,
    ) = refs[1 + LATE:]
    copies = [
        pltpu.make_async_copy(piece, table.at[(8 - LATE + k) * 1024:(9 - LATE + k) * 1024], sems.at[k])
        for k, piece in enumerate(late)
    ]

    def block_copies(b):
        rows = pl.ds(pl.multiple_of(b * SLOTS, SLOTS), SLOTS)
        return (
            pltpu.make_async_copy(far_edges_ref.at[rows], edges_buf, row_sems.at[0]),
            pltpu.make_async_copy(far_pre_ref.at[rows], pre_buf, row_sems.at[1]),
        )

    total = info_ref[TILES]
    for copy in copies:
        copy.start()

    @pl.when(total > 0)
    def _():
        for copy in block_copies(0):
            copy.start()

    agg[...] = agg_ref[...]
    inner_self = dot(nodes_ref[...].astype(BF16), w_self[...]) + bn1_ref[...]
    for copy in copies:
        copy.wait()

    def block(b, carry):
        @pl.when(b > 0)
        def _():
            for copy in block_copies(b):
                copy.start()

        count = jnp.minimum(SLOTS, (total - b * SLOTS + 15) // 16 * 16)

        row = b * (SLOTS // BLOCK)

        def gather(i, c):
            at, col, there = row + (i >> 4), (i & 15) * 16, pl.multiple_of(i * 64, 64)
            for k in range(16):
                rows_buf[pl.ds(there + k * 4, 4)] = table[code_ref[at, 0, col + k]].astype(F32)
            return c

        lax.fori_loop(0, count // 16, gather, 0)
        for copy in block_copies(b):
            copy.wait()
        valid = iota((SLOTS, 1), 0) + b * SLOTS < total
        sent = jnp.concatenate(
            [rows_buf[pl.ds(c, SLOTS, stride=4)] for c in range(4)], axis=1
        ).astype(BF16)
        pre = pre_buf[...] + dot(sent, w_sender[...])
        hidden = silu(pre).astype(BF16)
        update = layer_norm(dot(hidden, w2[...]) + b2_ref[...], gain_ref[...], shift_ref[...])
        update = jnp.where(valid, update, 0.0)
        new = jnp.where(valid, edges_buf[...].astype(F32) + update, 0.0)
        new_far[pl.ds(pl.multiple_of(b * SLOTS, SLOTS), SLOTS)] = new.astype(BF16)
        receivers = jnp.concatenate([rcv_ref[row + k] for k in range(SLOTS // BLOCK)], axis=1)
        hot = (iota((NODE, SLOTS), 0) == receivers).astype(BF16)
        agg[...] += dot(hot, update.astype(BF16))
        return carry

    blocks = (total + SLOTS - 1) // SLOTS
    lax.fori_loop(0, blocks, block, 0)
    new_far[pl.ds(pl.multiple_of(blocks * SLOTS, SLOTS), BLOCK)] = jnp.zeros((BLOCK, D), BF16)

    def store(t):
        rows = pl.ds(pl.multiple_of(t * TILE, TILE), TILE)
        return pltpu.make_async_copy(near.at[rows], new_edges_ref.at[rows], near_sems.at[t])

    def tile(t, carry):
        base = info_ref[t]
        end = info_ref[t + 1]
        first = base // BLOCK
        last = jnp.where(end > base, (end - 1) // BLOCK + 1, first)
        rows = pl.ds(pl.multiple_of(t * TILE, TILE), TILE)
        slots = jnp.concatenate([slot_ref[t]] * 8, axis=0).astype(F32)
        slots = jnp.transpose(slots, (1, 0)).astype(jnp.int32)[:, 0:1]

        start = base // 16 * 16
        fits = end - start <= BLOCK

        def scatter(start):
            hot = (iota((TILE, BLOCK), 1) + start == slots).astype(BF16)
            there = pl.ds(pl.multiple_of(start, 16), BLOCK)
            near[rows] = near[rows] + dot(hot, new_far[there]).astype(BF16)

        @pl.when(jnp.logical_and(end > base, fits))
        def _():
            scatter(start)

        @pl.when(jnp.logical_not(fits))
        def _():
            def some(b, c):
                scatter(b * BLOCK)
                return c

            lax.fori_loop(first, last, some, 0)

        store(t).start()
        return carry

    lax.fori_loop(0, TILES, tile, 0)
    inner = silu(inner_self + dot(agg[...].astype(BF16), w_aggr[...])).astype(BF16)
    out = layer_norm(dot(inner, wn2[...]) + bn2_ref[...], gain_n_ref[...], shift_n_ref[...])
    new_nodes_ref[...] = nodes_ref[...] + out
    for t in range(TILES):
        store(t).wait()


def full(shape):
    return pl.BlockSpec(shape, lambda *_: (0,) * len(shape))


ANY = pl.BlockSpec(memory_space=pl.ANY)
SMEM = pl.BlockSpec(memory_space=pltpu.SMEM)
VMEM = pl.BlockSpec(memory_space=pltpu.VMEM)
HBM = pl.BlockSpec(memory_space=pltpu.HBM)
ROW = pl.BlockSpec((1, 1, TILE), lambda t: (t, 0, 0))
EDGES = pl.BlockSpec((TILE, D), lambda t: (t, 0))
SQUARE = full((D, D))
VECTOR = full((1, D))


def kept(dims, kind):
    return pltpu.VMEM(dims, kind)


def keep(array):
    return pltpu.with_memory_space_constraint(array, pltpu.VMEM)


def far_away(array):
    return pltpu.with_memory_space_constraint(array, pltpu.HBM)


def shape(dims, kind):
    return jax.ShapeDtypeStruct(dims, kind)


def load_kernel(*refs):
    count = (len(refs) - 1) // 2
    copies = [pltpu.make_async_copy(refs[k], refs[count + k], refs[-1].at[k]) for k in range(count)]
    for copy in copies:
        copy.start()
    for copy in copies:
        copy.wait()


def load(*arrays):
    count = len(arrays)
    return pl.pallas_call(
        load_kernel,
        in_specs=[HBM] * count,
        out_specs=[VMEM] * count,
        out_shape=[kept(array.shape, array.dtype) for array in arrays],
        scratch_shapes=[pltpu.SemaphoreType.DMA((count,))],
        compiler_params=pltpu.CompilerParams(vmem_limit_bytes=16 << 20),
        cost_estimate=pl.CostEstimate(flops=0, bytes_accessed=16 << 20, transcendentals=0),
    )(*(far_away(array) for array in arrays))


def pick(spot, nodes, send_rows):
    return pl.pallas_call(
        pick_kernel,
        in_specs=[SMEM, HBM, HBM],
        out_specs=[VMEM] * 6,
        out_shape=(kept((NODE, D), F32), kept((NODE, D), BF16)) + (shape((HALO, D), BF16),) * 4,
        scratch_shapes=[pltpu.VMEM((4, HALO), jnp.int32), pltpu.SemaphoreType.DMA((2,))],
        compiler_params=pltpu.CompilerParams(vmem_limit_bytes=16 << 20),
        cost_estimate=pl.CostEstimate(flops=2 * NODE * D * 256, bytes_accessed=2 << 20, transcendentals=0),
    )(spot, far_away(nodes), far_away(send_rows))


def compact(*args):
    rows = BLOCKS * BLOCK
    return pl.pallas_call(
        compact_kernel,
        in_specs=[SMEM] + [VMEM] * (len(args) - 1),
        out_specs=[VMEM, SMEM, VMEM, VMEM, VMEM, VMEM, HBM, HBM],
        out_shape=(
            kept((TILES, 1, TILE), jnp.int32), shape((16,), jnp.int32),
            shape((BLOCKS, 1, BLOCK), jnp.int32), kept((BLOCKS, 1, BLOCK), jnp.int32),
            kept((NODE, D), BF16), kept((NODE, D), BF16),
            pltpu.HBM((rows, D), BF16), pltpu.HBM((rows, D), F32),
        ),
        scratch_shapes=[
            pltpu.VMEM((256, 256), BF16), pltpu.VMEM((rows, D), BF16),
            pltpu.VMEM((BLOCKS, 8, BLOCK), F32), pltpu.VMEM((rows, D), F32),
            pltpu.SMEM((1,), jnp.int32), pltpu.SemaphoreType.DMA((BLOCKS, 2)),
        ],
        compiler_params=pltpu.CompilerParams(vmem_limit_bytes=30 << 20),
        cost_estimate=pl.CostEstimate(flops=4 << 30, bytes_accessed=8 << 20, transcendentals=0),
    )(*args)


def near(begin, whole, half, pieces, *args):
    outs = [kept((EDGE, D), BF16), kept((NODE, D), F32)]
    scratch = [
        pltpu.VMEM((256, D), BF16), pltpu.VMEM((TILE, 1), jnp.int32), pltpu.VMEM((TILE, 1), jnp.int32),
        pltpu.VMEM((TILE, D), BF16),
    ]
    if begin == 0:
        outs = outs + [kept((NEAR, D), BF16)]
    if pieces:
        outs = outs + [kept((8192, 4, 128), BF16)]
        scratch = [pltpu.SemaphoreType.DMA((pieces,))] + scratch
    return pl.pallas_call(
        functools.partial(near_kernel, begin, whole, half, pieces),
        in_specs=[SMEM if k == 10 and begin == 0 else VMEM for k in range(len(args))],
        out_specs=[VMEM] * len(outs),
        out_shape=outs,
        scratch_shapes=scratch,
        input_output_aliases={11: 0, 12: 1} if begin else {},
        compiler_params=pltpu.CompilerParams(vmem_limit_bytes=16 << 20),
        cost_estimate=pl.CostEstimate(flops=(2 * whole + half) << 30, bytes_accessed=(2 * whole + half) << 20, transcendentals=0),
    )(*args)


def far(*args):
    return pl.pallas_call(
        far_kernel,
        in_specs=[SMEM] * 2 + [VMEM] + [ANY] * LATE + [VMEM] + [HBM] * 2 + [VMEM] * (len(args) - 6 - LATE),
        out_specs=[VMEM, ANY, VMEM, VMEM],
        out_shape=(shape((NODE, D), F32), shape((EDGE, D), BF16), kept((8192, 4, 128), BF16), kept((EDGE, D), BF16)),
        input_output_aliases={2: 2, 3 + LATE: 3},
        scratch_shapes=[
            pltpu.VMEM((4 * SLOTS, 128), F32),
            pltpu.VMEM((SLOTS, D), BF16), pltpu.VMEM((SLOTS, D), F32), pltpu.VMEM(((BLOCKS + 1) * BLOCK, D), BF16),
            pltpu.VMEM((NODE, D), F32),
            pltpu.SemaphoreType.DMA((LATE,)), pltpu.SemaphoreType.DMA((TILES,)), pltpu.SemaphoreType.DMA((2,)),
        ],
        compiler_params=pltpu.CompilerParams(vmem_limit_bytes=24 << 20),
        cost_estimate=pl.CostEstimate(flops=4 << 30, bytes_accessed=24 << 20, transcendentals=1 << 20),
    )(*args)


def body(
    nodes, edges, sender, receiver, send_rows,
    w_sender, w_receiver, w_edge, bias_edge1, w_edge2, bias_edge2, gain_edge, shift_edge,
    w_node_self, w_node_aggr, bias_node1, w_node2, bias_node2, gain_node, shift_node,
):
    row = lambda v: v.reshape(1, D)
    tiles = lambda v, size: v.reshape(EDGE // size, 1, size)
    after = lambda v, *first: lax.optimization_barrier((v,) + first)[0]
    x, c, y, z = (lax.axis_index(a) for a in AXES)
    spot = jnp.stack([x, y, z, c]).astype(jnp.int32)
    held = nodes[:COARSE_DEV].astype(BF16).reshape(COARSE_DEV, 4, 128)
    nodes, own, *out = pick(spot, nodes, send_rows)
    nodes, own = keep(nodes), keep(own)
    place = jnp.asarray(np.repeat(PLACES.reshape(2, 256), 16, axis=0), BF16)

    def grow(held, stage, *first):
        got = [from_chip(held, pair) for pair in stage]
        return jnp.concatenate([after(held, *first)] + got, axis=0)

    held = after(grow(held, STAGES[0]), own)
    halo = [shift_patch(after(out[0], held), 1), shift_patch(after(out[1], held), -1)]
    names = load(
        after(edges, held), tiles(sender, SUB), tiles(receiver, SUB), tiles(sender, TILE), tiles(receiver, TILE), w_sender, w_edge, w_edge2, w_receiver,
        w_node_self, w_node_aggr, w_node2,
        row(bias_edge1), row(bias_edge2), row(gain_edge), row(shift_edge),
        row(bias_node1), row(bias_node2), row(gain_node), row(shift_node), place,
    )
    (
        edges, snd, rcv, snd_t, rcv_t, w_sender, w_edge, w_edge2, w_receiver, w_node_self, w_node_aggr, w_node2,
        bias_edge1, *vectors, place,
    ) = (keep(v) for v in names)
    edge_vectors, node_vectors = vectors[:3], vectors[3:]

    def edge_part(begin, whole, half, pieces, *extra):
        outs = near(begin, whole, half, pieces, snd, rcv, edges, tr, w_edge, bias_edge1, w_edge2, *edge_vectors, *extra)
        return [keep(v) for v in outs]

    held = after(grow(held, STAGES[1]), edges, *halo)
    halo = halo + [next_chip(after(out[2], held)), other_core(after(out[3], held))]
    slot, info, far_code, far_rcv, own_ts, tr, far_edges, far_pre = compact(
        spot, snd_t, rcv_t, edges, keep(after(own, held)), w_sender, w_receiver, w_edge, bias_edge1, place,
    )
    slot, far_rcv, own_ts, tr = (keep(v) for v in (slot, far_rcv, own_ts, tr))
    held = grow(held, STAGES[2], tr, *halo)
    last = [from_chip(held, pair) for pair in LAST]
    done, agg, ts = edge_part(0, 2, 1, 0, spot, keep(after(own_ts, held)), *halo, w_sender)
    first = [other_core(held), other_core(after(last[0], agg))]
    done, agg = edge_part(5, 0, 1, 0, ts, done, agg)
    second = [other_core(after(piece, agg)) for piece in last[1:]]
    early = [held, *last, *first]
    done, agg, table = edge_part(6, 1, 0, 6, ts, done, agg, *early)
    new_nodes, new_edges, _, _ = far(
        info, far_code, table, *second, done,
        far_away(far_edges), far_away(far_pre), agg, slot, far_rcv, nodes,
        w_sender, w_edge2, w_node_self, w_node_aggr, w_node2, *edge_vectors, *node_vectors,
    )
    return new_nodes, new_edges


def solution(mesh):
    grid = Mesh(mesh.devices.reshape(SIZES), AXES)
    split = P(AXES, None)
    return jax.shard_map(
        body,
        mesh=grid,
        in_specs=(split, split, P(AXES), P(AXES), split) + (P(),) * 15,
        out_specs=(split, split),
        check_vma=False,
    )
```
